512 devices in a mesh: replica: 16 (over z, y_lo), fsdp: 32 (over y_hi, x, core).
Axes of the slice: x: 4, y: 8 (y_hi: 4, y_lo: 2; y = y_hi * 2 + y_lo), z: 8, core: 2. Of those that a mesh axis runs over, the one named last changes fastest.
Arguments:
- inputs: bfloat16 [16, 12288, 4096], P('replica', 'fsdp'), may hold values from -6 to 6
- feature_gain: float32 [4096], replicated, may hold values from 0.7 to 14
- key_weight: bfloat16 [16, 4096, 512], P('replica', 'fsdp'), may hold values from -0.09375 to 0.09375
- teacher_keys: bfloat16 [16, 12288, 512], P('replica', 'fsdp'), may hold values from -40 to 40
- global_frag: bfloat16 [4194304], P('fsdp'), may hold values from -6 to 6
- local_frag: bfloat16 [16, 4194304], P('replica', 'fsdp'), may hold values from -6 to 6
- momentum: float32 [4194304], P(('fsdp', 'replica')), may hold values from -3 to 3
Outputs:
- clipped_grad: bfloat16 [16, 4096, 512], P('replica', 'fsdp')
- new_global: bfloat16 [4194304], P('fsdp')
- new_momentum: float32 [4194304], P(('fsdp', 'replica'))
The draws below stay inside these ranges and needn't reach their ends.
All inputs are finite; a program needn't handle non-finite values.
Results may differ from the reference program's by a relative error of at most 0.027.
Values may be sent and summed in bfloat16 or wider, within the bound.
No kernel may reach another device: no remote copies, remote signals or barrier semaphores. Data moves between devices by JAX's collectives and lax.ppermute only.
A program may use at most 64 MiB of HBM per device.

```python
import math
import jax
import jax.numpy as jnp
from jax import lax

DW = 4096
KW = 512
TOK_DEV = 384
QBLOCK = 128
REPLICAS = 16
TOKENS = 12288
FRAG = 4194304
N_FSDP = 32


def draw_feature_gain(key, part):
    key = jax.random.fold_in(key, 11)
    ramp = jnp.arange(DW).astype(jnp.float32) / (DW - 1)
    rough = jax.random.uniform(key, (DW,), jnp.float32, math.log(0.7), math.log(1.4))
    return jnp.exp(math.log(10.0) * ramp + rough)


def draw_teacher_keys(key, part):
    key = jax.random.fold_in(key, 23)
    first_key = jax.random.fold_in(key, 0)
    third_key = jax.random.fold_in(key, 2)
    columns = jnp.exp(jax.random.uniform(first_key, (KW,), jnp.float32, 0.0, math.log(10.0)))
    noise = jnp.clip(jax.random.normal(third_key, (REPLICAS, TOKENS, KW), jnp.float32), -4.0, 4.0)
    return (noise * columns).astype(jnp.bfloat16)


def strengthened(values, key, source, target, parts, factor):
    def block_of(position):
        return (jnp.arange(values.shape[position]) // (values.shape[position] // parts)).reshape((-1,) + (1,) * (values.ndim - 1 - position))

    one_side = jax.random.permutation(key, parts)[block_of(target)]
    other_side = (block_of(target) + parts // 2) % parts
    return jnp.where((block_of(source) == one_side) | (block_of(source) == other_side), factor * values, values)


def block_levels(own_key, shape, shards, smallest, top_value):
    def one(position, parts):
        steps = jax.random.uniform(jax.random.fold_in(jax.random.fold_in(own_key, 6), position), (parts,), jnp.float32, smallest / len(shards), top_value / len(shards))
        return jnp.repeat(jnp.exp(steps), shape[position] // parts).reshape((-1,) + (1,) * (len(shape) - position - 1))

    gain = one(*shards[0])
    for cut in shards[1:]:
        gain = gain * one(*cut)
    return gain


def bell_draw(own_key, shape, spread, limit, cuts=(), held_as=jnp.bfloat16):
    result = spread * jax.random.normal(own_key, shape, jnp.float32)
    if cuts:
        result = result * block_levels(own_key, shape, cuts, -0.22, 0.18)
    return jnp.clip(result, -limit, limit).astype(held_as)


def bell_draw_with(stream_key, dims, width, limit, pieces, heavy, kind=jnp.bfloat16):
    values = width * jax.random.normal(stream_key, dims, jnp.float32)
    if pieces:
        values = values * block_levels(stream_key, dims, pieces, -0.22, 0.18)
    return jnp.clip(strengthened(values, jax.random.fold_in(stream_key, 3), *heavy), -limit, limit).astype(kind)


def setup_inputs(seed: int = 0) -> dict:
    splits = jax.random.split(jax.random.key(seed), 8)
    return {
        "inputs": bell_draw_with(splits[0], (REPLICAS, TOKENS, DW), 1.0, 6.0, ((0, 16), (1, 32)), (1, 2, 32, 2.75)),
        "feature_gain": draw_feature_gain(jax.random.fold_in(splits[7], 71), 0),
        "key_weight": bell_draw(splits[2], (REPLICAS, DW, KW), DW ** -0.5, 0.09375, ((0, 16), (1, 32))),
        "teacher_keys": draw_teacher_keys(jax.random.fold_in(splits[7], 71), 0),
        "global_frag": bell_draw(splits[4], (FRAG,), 1.0, 6.0, ((0, 32),)),
        "local_frag": bell_draw_with(splits[5], (REPLICAS, FRAG), 1.0, 6.0, ((0, 16), (1, 32)), (0, 1, 16, 2.0)),
        "momentum": bell_draw(splits[6], (FRAG,), 0.5, 3.0, ((0, 512),), jnp.float32),
    }


outer_decay = 0.9
outer_rate = 0.7
clip_ratio = 2.0
epsilon = 1e-06

def inner_gradient(replica_inputs, feature_gain, replica_weight, replica_targets):
    scaled = (replica_inputs.astype(jnp.float32) * feature_gain[None, :]).astype(jnp.bfloat16)
    projected = jnp.dot(scaled, replica_weight, preferred_element_type=jnp.float32)
    residual = (projected - replica_targets.astype(jnp.float32)).astype(jnp.bfloat16)
    scaled_blocks = scaled.reshape(N_FSDP, TOK_DEV, scaled.shape[1])
    residual_blocks = residual.reshape(N_FSDP, TOK_DEV, residual.shape[1])

    def add_block(running, block_pair):
        term = jnp.dot(block_pair[0].T, block_pair[1], preferred_element_type=jnp.float32)
        rounded = lax.optimization_barrier(term.astype(jnp.bfloat16))
        return (running + rounded.astype(jnp.float32), None)
    zero_sum = jnp.zeros((scaled.shape[1], residual.shape[1]), jnp.float32)
    gradient, unused = lax.scan(add_block, zero_sum, (scaled_blocks, residual_blocks))
    mean_square = jnp.sum(gradient * gradient) / (gradient.shape[0] * gradient.shape[1])
    factor = jnp.minimum(1.0, lax.rsqrt(mean_square + epsilon))
    return (gradient * factor).astype(jnp.bfloat16)

def encode(difference):
    blocks = difference.reshape(difference.shape[:-1] + (-1, QBLOCK))
    scales = (clip_ratio * jnp.sqrt(lax.optimization_barrier(jnp.mean(blocks * blocks, axis=-1)) + epsilon)).astype(jnp.bfloat16)
    block_codes = jnp.clip(blocks / scales.astype(jnp.float32)[..., None], -1.0, 1.0).astype(jnp.bfloat16)
    return (block_codes, scales)

def reference(inputs, feature_gain, key_weight, teacher_keys, global_frag, local_frag, momentum):

    def one_replica(replica_trio):
        return inner_gradient(replica_trio[0], feature_gain, replica_trio[1], replica_trio[2])
    clipped_grad = lax.map(one_replica, (inputs, key_weight, teacher_keys))
    global_values = global_frag.astype(jnp.float32)

    def add_replica(running, local_row):
        block_codes, scales = encode(global_values - local_row.astype(jnp.float32))
        decoded = block_codes.astype(jnp.float32) * scales.astype(jnp.float32)[:, None]
        return (running + decoded.reshape(-1), None)
    summed, unused = lax.scan(add_replica, jnp.zeros_like(global_values), local_frag)
    pseudo = summed / REPLICAS
    new_momentum = outer_decay * momentum + pseudo
    new_global = (global_values - outer_rate * (pseudo + outer_decay * new_momentum)).astype(jnp.bfloat16)
    return (clipped_grad, new_global, new_momentum)
```

```python
import jax
import jax.numpy as jnp
from jax import lax
from jax.sharding import Mesh
from jax.sharding import PartitionSpec as P

QBLOCK = 128


outer_decay = 0.9
outer_rate = 0.7
clip_ratio = 2.0
epsilon = 1e-06

AXES = {"z": 8, "y_lo": 2, "y_hi": 4, "x": 4, "core": 2}
REPLICA = ("z", "y_lo")
FSDP = ("y_hi", "x", "core")


def encode(difference):
    blocks = difference.reshape(-1, QBLOCK)
    scales = (clip_ratio * jnp.sqrt(jnp.mean(blocks * blocks, axis=-1) + epsilon)).astype(
        jnp.bfloat16
    )
    block_codes = jnp.clip(blocks / scales.astype(jnp.float32)[:, None], -1.0, 1.0).astype(
        jnp.bfloat16
    )
    return (block_codes, scales)


def exchange_sum(parts, axis):
    arrived = lax.all_to_all(parts, axis, split_axis=0, concat_axis=0, tiled=True)
    return jnp.sum(arrived.astype(jnp.float32), axis=0)


def fragment_update(global_frag, local_frag, momentum):
    global_values = global_frag.astype(jnp.float32)
    block_codes, scales = encode(global_values - local_frag[0].astype(jnp.float32))
    decoded = (
        block_codes.astype(jnp.float32) * scales.astype(jnp.float32)[:, None]
    ).astype(jnp.bfloat16)
    replicas = AXES["z"] * AXES["y_lo"]
    share = global_frag.shape[0] // replicas
    rows = share // QBLOCK
    pseudo = exchange_sum(decoded.reshape(replicas, rows, QBLOCK), REPLICA) / replicas
    new_momentum = outer_decay * momentum.reshape(rows, QBLOCK) + pseudo
    offset = lax.axis_index(REPLICA) * share
    own_global = lax.dynamic_slice_in_dim(global_frag, offset, share).reshape(rows, QBLOCK)
    own_next = (
        own_global.astype(jnp.float32) - outer_rate * (pseudo + outer_decay * new_momentum)
    ).astype(jnp.bfloat16)
    new_global = lax.all_to_all(
        jnp.broadcast_to(own_next[None], (replicas, rows, QBLOCK)),
        REPLICA,
        split_axis=0,
        concat_axis=0,
        tiled=True,
    )
    return new_global.reshape(-1), new_momentum.reshape(-1)


def shards(inputs, feature_gain, key_weight, teacher_keys, global_frag, local_frag, momentum):
    tokens, features = inputs.shape[1:]
    rows, width = key_weight.shape[1:]
    scaled = (inputs[0].astype(jnp.float32) * feature_gain[None, :]).astype(jnp.bfloat16)
    by_owner = lax.optimization_barrier(
        scaled.reshape(tokens, AXES["y_hi"], AXES["x"], AXES["core"], rows)
        .transpose(0, 3, 2, 1, 4)
        .reshape(tokens, features)
    )
    new_global, new_momentum = fragment_update(global_frag, local_frag, momentum)
    projected = jnp.dot(
        scaled,
        lax.all_gather(key_weight[0], FSDP, axis=0, tiled=True),
        preferred_element_type=jnp.float32,
    )
    residual = (projected - teacher_keys[0].astype(jnp.float32)).astype(jnp.bfloat16)
    partial = lax.dot_general(
        by_owner, residual, (((0,), (0,)), ((), ())), preferred_element_type=jnp.float32
    )
    for axis in ("core", "x", "y_hi"):
        partial = exchange_sum(
            partial.astype(jnp.bfloat16).reshape(AXES[axis], -1, width), axis
        )
    gradient = partial
    squares = jnp.sum(gradient * gradient)
    spread = lax.all_to_all(
        jnp.full((lax.axis_size(FSDP), 1), squares), FSDP, split_axis=0, concat_axis=0, tiled=True
    )
    factor = jnp.minimum(1.0, lax.rsqrt(jnp.sum(spread) / (features * width) + epsilon))
    clipped_grad = (gradient * factor).astype(jnp.bfloat16)[None]
    return (clipped_grad, new_global, new_momentum)


def solution(mesh):
    parted = Mesh(mesh.devices.reshape(tuple(AXES.values())), tuple(AXES))
    return jax.shard_map(
        shards,
        mesh=parted,
        in_specs=(
            P(REPLICA, FSDP, None),
            P(),
            P(REPLICA, FSDP, None),
            P(REPLICA, FSDP, None),
            P(FSDP),
            P(REPLICA, FSDP),
            P(FSDP + REPLICA),
        ),
        out_specs=(P(REPLICA, FSDP, None), P(FSDP), P(FSDP + REPLICA)),
        check_vma=False,
    )
```

```python
import functools

import jax
import jax.numpy as jnp
from jax import lax
from jax.experimental import pallas as pl
from jax.experimental.pallas import tpu as pltpu
from jax.sharding import Mesh
from jax.sharding import PartitionSpec as P

QBLOCK = 128
LANES = 128


outer_decay = 0.9
outer_rate = 0.7
clip_ratio = 2.0
epsilon = 1e-06

AXES = {"z": 8, "y_lo": 2, "y_hi": 4, "x": 4, "core": 2}
REPLICA = ("z", "y_lo")
FSDP = ("y_hi", "x", "core")
CHIPS = AXES["x"] * AXES["y_hi"]
X_FIRST = 384


def encode(difference):
    blocks = difference.reshape(-1, QBLOCK)
    scales = (clip_ratio * jnp.sqrt(jnp.mean(blocks * blocks, axis=-1) + epsilon)).astype(
        jnp.bfloat16
    )
    block_codes = jnp.clip(blocks / scales.astype(jnp.float32)[:, None], -1.0, 1.0).astype(
        jnp.bfloat16
    )
    return (block_codes, scales)


def send(value, axis, step):
    size = AXES[axis]
    return lax.ppermute(value, axis, [(i, (i + step) % size) for i in range(size)])


def tied(*values):
    return lax.optimization_barrier(values)


def arrange_kernel(order_ref, inputs_ref, gain_ref, own_ref, other_ref):
    for half, out_ref in enumerate((own_ref, other_ref)):
        for j in range(CHIPS):
            start = pl.multiple_of(order_ref[half * CHIPS + j] * LANES, LANES)
            columns = pl.ds(start, LANES)
            out_ref[:, j * LANES : (j + 1) * LANES] = (
                inputs_ref[:, columns].astype(jnp.float32) * gain_ref[:, columns]
            ).astype(jnp.bfloat16)


def arrange(inputs, feature_gain):
    tokens, features = inputs.shape
    x, y, core = (lax.axis_index(name) for name in ("x", "y_hi", "core"))
    rx, ry = jnp.arange(CHIPS) // AXES["y_hi"], jnp.arange(CHIPS) % AXES["y_hi"]
    chip = (y + ry) % AXES["y_hi"] * AXES["x"] + (x + rx) % AXES["x"]
    order = jnp.concatenate([chip * 2 + core, chip * 2 + 1 - core]).astype(jnp.int32)
    half = jax.ShapeDtypeStruct((tokens, features // 2), jnp.bfloat16)
    return pl.pallas_call(
        arrange_kernel,
        out_shape=(half, half),
        in_specs=[
            pl.BlockSpec(memory_space=pltpu.SMEM),
            pl.BlockSpec(memory_space=pltpu.VMEM),
            pl.BlockSpec(memory_space=pltpu.VMEM),
        ],
        out_specs=(pl.BlockSpec(memory_space=pltpu.VMEM),) * 2,
        compiler_params=pltpu.CompilerParams(vmem_limit_bytes=24 << 20),
        name="arrange",
    )(order, inputs, feature_gain[None, :])


def fragment_sum(global_frag, local_frag):
    difference = global_frag.astype(jnp.float32) - local_frag.astype(jnp.float32)
    block_codes, scales = encode(difference)
    decoded = (
        block_codes.astype(jnp.float32) * scales.astype(jnp.float32)[:, None]
    ).astype(jnp.bfloat16)
    replicas = AXES["z"] * AXES["y_lo"]
    arrived = lax.all_to_all(
        decoded.reshape(replicas, -1, QBLOCK), REPLICA, split_axis=0, concat_axis=0, tiled=True
    )
    return arrived


def fragment_update(arrived, global_frag, momentum):
    replicas, rows = arrived.shape[:2]
    share = rows * QBLOCK
    pseudo = jnp.sum(arrived.astype(jnp.float32), axis=0) / replicas
    new_momentum = outer_decay * momentum.reshape(rows, QBLOCK) + pseudo
    offset = lax.axis_index(REPLICA) * share
    own_global = lax.dynamic_slice_in_dim(global_frag, offset, share).reshape(rows, QBLOCK)
    own_next = (
        own_global.astype(jnp.float32) - outer_rate * (pseudo + outer_decay * new_momentum)
    ).astype(jnp.bfloat16)
    new_global = lax.all_to_all(
        jnp.broadcast_to(own_next[None], (replicas, rows, QBLOCK)),
        REPLICA,
        split_axis=0,
        concat_axis=0,
        tiled=True,
    )
    return new_global.reshape(-1), new_momentum.reshape(-1)


def total(values):
    return functools.reduce(jnp.add, [value.astype(jnp.float32) for value in values])


def shards(inputs, feature_gain, key_weight, teacher_keys, global_frag, local_frag, momentum):
    features = inputs.shape[2]
    rows, width = key_weight.shape[1:]
    steps = (2, 1, 3)

    weight = key_weight[0]
    parts = [weight[:, :X_FIRST], weight[:, X_FIRST:]]
    axes = [("y_hi", "x"), ("x", "y_hi")]
    near = [{0: part} | {k: send(part, a[0], -k) for k in steps} for part, a in zip(parts, axes)]
    own, other = arrange(inputs[0], feature_gain)
    scaled = jnp.concatenate([own, send(other, "core", 1)], axis=0)
    targets = jnp.concatenate([teacher_keys[0], send(teacher_keys[0], "core", 1)], axis=0)
    arrived = fragment_sum(global_frag, local_frag[0])
    near = [jnp.stack([n[k] for k in range(4)]) for n in near]
    far = [{0: n} | {k: send(n, a[1], -k) for k in steps} for n, a in zip(near, axes)]
    far = [jnp.stack([f[k] for k in range(4)]) for f in far]
    gathered = jnp.concatenate(
        [
            far[0].reshape(CHIPS * rows, X_FIRST),
            far[1].transpose(1, 0, 2, 3).reshape(CHIPS * rows, width - X_FIRST),
        ],
        axis=1,
    )
    gathered, arrived, scaled, targets = tied(gathered, arrived, scaled, targets)

    partial = jnp.dot(scaled, gathered, preferred_element_type=jnp.float32)
    tokens = inputs.shape[1]
    theirs = send(partial, "core", 1)
    projected = partial + jnp.concatenate([theirs[tokens:], theirs[:tokens]], axis=0)
    residual = (projected - targets.astype(jnp.float32)).astype(jnp.bfloat16)

    def product(columns, targets):
        return lax.dot_general(
            columns, targets, (((0,), (0,)), ((), ())), preferred_element_type=jnp.float32
        ).astype(jnp.bfloat16)

    by_y = (
        product(scaled, residual[:, X_FIRST:])
        .reshape(AXES["x"], AXES["y_hi"], rows, width - X_FIRST)
        .transpose(1, 0, 2, 3)
    )
    group = scaled.shape[1] // AXES["x"]
    by_x = [
        product(scaled[:, k * group : (k + 1) * group], residual[:, :X_FIRST]).reshape(
            AXES["y_hi"], rows, X_FIRST
        )
        for k in range(4)
    ]
    sums = []
    first_x = [by_x[0]] + [send(by_x[k], "x", k) for k in steps]
    first_y = [by_y[0]] + [send(by_y[k], "y_hi", k) for k in steps]
    arrived, first_x[0] = tied(arrived, first_x[0])
    new_global, new_momentum = fragment_update(arrived, global_frag, momentum)
    first_x, first_y, new_global = tied(first_x, first_y, new_global)
    second = [total(first_x).astype(jnp.bfloat16), total(first_y).astype(jnp.bfloat16)]
    for value, axis in zip(second, ("y_hi", "x")):
        sums.append(total([value[0]] + [send(value[k], axis, k) for k in steps]))
    gradient = jnp.concatenate(sums, axis=1)

    squares = jnp.sum(gradient * gradient)
    spread = lax.all_to_all(
        jnp.full((lax.axis_size(FSDP), 1), squares), FSDP, split_axis=0, concat_axis=0, tiled=True
    )
    factor = jnp.minimum(1.0, lax.rsqrt(jnp.sum(spread) / (features * width) + epsilon))
    clipped_grad = (gradient * factor).astype(jnp.bfloat16)[None]
    return (clipped_grad, new_global, new_momentum)


def solution(mesh):
    parted = Mesh(mesh.devices.reshape(tuple(AXES.values())), tuple(AXES))
    return jax.shard_map(
        shards,
        mesh=parted,
        in_specs=(
            P(REPLICA, FSDP, None),
            P(),
            P(REPLICA, FSDP, None),
            P(REPLICA, FSDP, None),
            P(FSDP),
            P(REPLICA, FSDP),
            P(FSDP + REPLICA),
        ),
        out_specs=(P(REPLICA, FSDP, None), P(FSDP), P(FSDP + REPLICA)),
        check_vma=False,
    )
```

```python
import jax
import jax.numpy as jnp
from jax import lax
from jax.experimental import pallas as pl
from jax.experimental.pallas import tpu as pltpu
from jax.sharding import Mesh
from jax.sharding import PartitionSpec as P

QBLOCK = 128
LANES = 128


outer_decay = 0.9
outer_rate = 0.7
clip_ratio = 2.0
epsilon = 1e-06

AXES = {"z": 8, "y_lo": 2, "y_hi": 4, "x": 4, "core": 2}
REPLICA = ("z", "y_lo")
FSDP = ("y_hi", "x", "core")
CHIPS = AXES["x"] * AXES["y_hi"]


def encode(difference):
    blocks = difference.reshape(-1, QBLOCK)
    scales = (clip_ratio * jnp.sqrt(jnp.mean(blocks * blocks, axis=-1) + epsilon)).astype(
        jnp.bfloat16
    )
    block_codes = jnp.clip(blocks / scales.astype(jnp.float32)[:, None], -1.0, 1.0).astype(
        jnp.bfloat16
    )
    return (block_codes, scales)


def send(value, axis, step):
    size = AXES[axis]
    return lax.ppermute(value, axis, [(i, (i + step) % size) for i in range(size)])


def tied(*values):
    return lax.optimization_barrier(values)


def arrange_kernel(order_ref, inputs_ref, gain_ref, own_ref, other_ref):
    for half, out_ref in enumerate((own_ref, other_ref)):
        for j in range(CHIPS):
            start = pl.multiple_of(order_ref[half * CHIPS + j] * LANES, LANES)
            columns = pl.ds(start, LANES)
            out_ref[:, j * LANES : (j + 1) * LANES] = (
                inputs_ref[:, columns].astype(jnp.float32) * gain_ref[:, columns]
            ).astype(jnp.bfloat16)


def arrange(inputs, feature_gain):
    tokens, features = inputs.shape
    core = lax.axis_index("core")
    chip = jnp.arange(CHIPS) % AXES["y_hi"] * AXES["x"] + jnp.arange(CHIPS) // AXES["y_hi"]
    order = jnp.concatenate([chip * 2 + core, chip * 2 + 1 - core]).astype(jnp.int32)
    half = jax.ShapeDtypeStruct((tokens, features // 2), jnp.bfloat16)
    return pl.pallas_call(
        arrange_kernel,
        out_shape=(half, half),
        in_specs=[
            pl.BlockSpec(memory_space=pltpu.SMEM),
            pl.BlockSpec(memory_space=pltpu.VMEM),
            pl.BlockSpec(memory_space=pltpu.VMEM),
        ],
        out_specs=(pl.BlockSpec(memory_space=pltpu.VMEM),) * 2,
        compiler_params=pltpu.CompilerParams(vmem_limit_bytes=24 << 20),
        name="arrange",
    )(order, inputs, feature_gain[None, :])


def exchange(parts, axis):
    return lax.all_to_all(parts, axis, split_axis=0, concat_axis=0, tiled=True)


def spread(value, axis):
    return exchange(jnp.broadcast_to(value[None], (lax.axis_size(axis), *value.shape)), axis)


def total(arrived):
    return jnp.sum(arrived.astype(jnp.float32), axis=0)


def fragment_codes(global_frag, local_frag):
    difference = global_frag.astype(jnp.float32) - local_frag.astype(jnp.float32)
    block_codes, scales = encode(difference)
    decoded = block_codes.astype(jnp.float32) * scales.astype(jnp.float32)[:, None]
    return decoded.astype(jnp.bfloat16).reshape(lax.axis_size(REPLICA), -1, QBLOCK)


def fragment_update(decoded, global_frag, momentum):
    replicas, rows = decoded.shape[:2]
    share = rows * QBLOCK
    pseudo = total(exchange(decoded, REPLICA)) / replicas
    new_momentum = outer_decay * momentum.reshape(rows, QBLOCK) + pseudo
    offset = lax.axis_index(REPLICA) * share
    own_global = lax.dynamic_slice_in_dim(global_frag, offset, share).reshape(rows, QBLOCK)
    own_next = (
        own_global.astype(jnp.float32) - outer_rate * (pseudo + outer_decay * new_momentum)
    ).astype(jnp.bfloat16)
    return spread(own_next, REPLICA).reshape(-1), new_momentum.reshape(-1)


def shards(inputs, feature_gain, key_weight, teacher_keys, global_frag, local_frag, momentum):
    tokens, features = inputs.shape[1:]
    rows, width = key_weight.shape[1:]

    column = spread(key_weight[0], "y_hi")
    own, other = arrange(inputs[0], feature_gain)
    decoded = fragment_codes(global_frag, local_frag[0])
    column, own, other, decoded = tied(column, own, other, decoded)
    gathered = lax.all_gather(
        column.reshape(AXES["y_hi"] * rows, width), "x", axis=0, tiled=True
    )
    scaled = jnp.concatenate([own, send(other, "core", 1)], axis=0)
    targets = jnp.concatenate([teacher_keys[0], send(teacher_keys[0], "core", 1)], axis=0)
    new_global, new_momentum = fragment_update(decoded, global_frag, momentum)
    gathered, new_global, scaled, targets = tied(gathered, new_global, scaled, targets)

    partial = jnp.dot(scaled, gathered, preferred_element_type=jnp.float32)
    theirs = send(partial, "core", 1)
    projected = partial + jnp.concatenate([theirs[tokens:], theirs[:tokens]], axis=0)
    residual = (projected - targets.astype(jnp.float32)).astype(jnp.bfloat16)
    gradient = lax.dot_general(
        scaled, residual, (((0,), (0,)), ((), ())), preferred_element_type=jnp.float32
    )
    for axis in ("x", "y_hi"):
        gradient = total(
            exchange(gradient.astype(jnp.bfloat16).reshape(AXES[axis], -1, width), axis)
        )

    squares = jnp.sum(gradient * gradient)
    mean_square = jnp.sum(spread(squares[None], FSDP)) / (features * width)
    factor = jnp.minimum(1.0, lax.rsqrt(mean_square + epsilon))
    clipped_grad = (gradient * factor).astype(jnp.bfloat16)[None]
    return (clipped_grad, new_global, new_momentum)


def solution(mesh):
    parted = Mesh(mesh.devices.reshape(tuple(AXES.values())), tuple(AXES))
    return jax.shard_map(
        shards,
        mesh=parted,
        in_specs=(
            P(REPLICA, FSDP, None),
            P(),
            P(REPLICA, FSDP, None),
            P(REPLICA, FSDP, None),
            P(FSDP),
            P(REPLICA, FSDP),
            P(FSDP + REPLICA),
        ),
        out_specs=(P(REPLICA, FSDP, None), P(FSDP), P(FSDP + REPLICA)),
        check_vma=False,
    )
```

```python
import functools

import jax
import jax.numpy as jnp
from jax import lax
from jax.experimental import pallas as pl
from jax.experimental.pallas import tpu as pltpu
from jax.sharding import Mesh
from jax.sharding import PartitionSpec as P

QBLOCK = 128
LANES = 128


outer_decay = 0.9
outer_rate = 0.7
clip_ratio = 2.0
epsilon = 1e-06

AXES = {"z": 8, "y_lo": 2, "y_hi": 4, "x": 4, "core": 2}
REPLICA = ("z", "y_lo")
FSDP = ("y_hi", "x", "core")
CHIPS = AXES["x"] * AXES["y_hi"]
STEPS = (2, 1, 3)


def encode(difference):
    blocks = difference.reshape(-1, QBLOCK)
    scales = (clip_ratio * jnp.sqrt(jnp.mean(blocks * blocks, axis=-1) + epsilon)).astype(
        jnp.bfloat16
    )
    block_codes = jnp.clip(blocks / scales.astype(jnp.float32)[:, None], -1.0, 1.0).astype(
        jnp.bfloat16
    )
    return (block_codes, scales)


def send(value, axis, step):
    size = AXES[axis]
    return lax.ppermute(value, axis, [(i, (i + step) % size) for i in range(size)])


def tied(*values):
    return lax.optimization_barrier(values)


def arrange_kernel(order_ref, inputs_ref, gain_ref, own_ref, other_ref):
    for half, out_ref in enumerate((own_ref, other_ref)):
        for j in range(CHIPS):
            start = pl.multiple_of(order_ref[half * CHIPS + j] * LANES, LANES)
            columns = pl.ds(start, LANES)
            out_ref[:, j * LANES : (j + 1) * LANES] = (
                inputs_ref[:, columns].astype(jnp.float32) * gain_ref[:, columns]
            ).astype(jnp.bfloat16)


def arrange(inputs, feature_gain):
    tokens, features = inputs.shape
    x, y, core = (lax.axis_index(name) for name in ("x", "y_hi", "core"))
    rx, ry = jnp.arange(CHIPS) // AXES["y_hi"], jnp.arange(CHIPS) % AXES["y_hi"]
    chip = (y + ry) % AXES["y_hi"] * AXES["x"] + (x + rx) % AXES["x"]
    order = jnp.concatenate([chip * 2 + core, chip * 2 + 1 - core]).astype(jnp.int32)
    half = jax.ShapeDtypeStruct((tokens, features // 2), jnp.bfloat16)
    return pl.pallas_call(
        arrange_kernel,
        out_shape=(half, half),
        in_specs=[
            pl.BlockSpec(memory_space=pltpu.SMEM),
            pl.BlockSpec(memory_space=pltpu.VMEM),
            pl.BlockSpec(memory_space=pltpu.VMEM),
        ],
        out_specs=(pl.BlockSpec(memory_space=pltpu.VMEM),) * 2,
        compiler_params=pltpu.CompilerParams(vmem_limit_bytes=24 << 20),
        name="arrange",
    )(order, inputs, feature_gain[None, :])


def exchange(parts, axis):
    return lax.all_to_all(parts, axis, split_axis=0, concat_axis=0, tiled=True)


def spread(value, axis):
    return exchange(jnp.broadcast_to(value[None], (lax.axis_size(axis), *value.shape)), axis)


def total(values):
    return functools.reduce(jnp.add, [value.astype(jnp.float32) for value in values])


def fragment_codes(global_frag, local_frag):
    difference = global_frag.astype(jnp.float32) - local_frag.astype(jnp.float32)
    block_codes, scales = encode(difference)
    decoded = block_codes.astype(jnp.float32) * scales.astype(jnp.float32)[:, None]
    return decoded.astype(jnp.bfloat16).reshape(lax.axis_size(REPLICA), -1, QBLOCK)


def fragment_update(arrived, global_frag, momentum):
    replicas, rows = arrived.shape[:2]
    share = rows * QBLOCK
    pseudo = jnp.sum(arrived.astype(jnp.float32), axis=0) / replicas
    new_momentum = outer_decay * momentum.reshape(rows, QBLOCK) + pseudo
    offset = lax.axis_index(REPLICA) * share
    own_global = lax.dynamic_slice_in_dim(global_frag, offset, share).reshape(rows, QBLOCK)
    own_next = (
        own_global.astype(jnp.float32) - outer_rate * (pseudo + outer_decay * new_momentum)
    ).astype(jnp.bfloat16)
    return spread(own_next, REPLICA).reshape(-1), new_momentum.reshape(-1)


def shards(inputs, feature_gain, key_weight, teacher_keys, global_frag, local_frag, momentum):
    tokens, features = inputs.shape[1:]
    rows, width = key_weight.shape[1:]

    weight = key_weight[0]
    near = [weight] + [None] * 3
    for k in STEPS:
        near[k] = send(weight, "y_hi", -k)
    arrived = exchange(fragment_codes(global_frag, local_frag[0]), REPLICA)
    column = jnp.concatenate(near, axis=0)
    own, other = arrange(inputs[0], feature_gain)
    column, arrived, own, other = tied(column, arrived, own, other)
    far = {k: send(column, "x", -k) for k in STEPS}
    scaled = jnp.concatenate([own, send(other, "core", 1)], axis=0)
    targets = jnp.concatenate([teacher_keys[0], send(teacher_keys[0], "core", 1)], axis=0)
    scaled, targets = tied(scaled, targets)
    group = scaled.shape[1] // AXES["x"]
    blocks = [scaled[:, k * group : (k + 1) * group] for k in range(AXES["x"])]
    partial = jnp.dot(blocks[0], column, preferred_element_type=jnp.float32)
    new_global, new_momentum = fragment_update(arrived, global_frag, momentum)
    for k in STEPS:
        partial += jnp.dot(blocks[k], far[k], preferred_element_type=jnp.float32)
    partial, new_global = tied(partial, new_global)

    theirs = send(partial, "core", 1)
    projected = partial + jnp.concatenate([theirs[tokens:], theirs[:tokens]], axis=0)
    residual = (projected - targets.astype(jnp.float32)).astype(jnp.bfloat16)
    gradient = [
        lax.dot_general(
            block, residual, (((0,), (0,)), ((), ())), preferred_element_type=jnp.float32
        ).astype(jnp.bfloat16)
        for block in blocks
    ]
    mine = total([gradient[0]] + [send(gradient[k], "x", k) for k in STEPS])
    mine = mine.astype(jnp.bfloat16).reshape(AXES["y_hi"], rows, width)
    gradient = total([mine[0]] + [send(mine[k], "y_hi", k) for k in STEPS])

    squares = jnp.sum(gradient * gradient)
    mean_square = jnp.sum(spread(squares[None], FSDP)) / (features * width)
    factor = jnp.minimum(1.0, lax.rsqrt(mean_square + epsilon))
    clipped_grad = (gradient * factor).astype(jnp.bfloat16)[None]
    return (clipped_grad, new_global, new_momentum)


def solution(mesh):
    parted = Mesh(mesh.devices.reshape(tuple(AXES.values())), tuple(AXES))
    return jax.shard_map(
        shards,
        mesh=parted,
        in_specs=(
            P(REPLICA, FSDP, None),
            P(),
            P(REPLICA, FSDP, None),
            P(REPLICA, FSDP, None),
            P(FSDP),
            P(REPLICA, FSDP),
            P(FSDP + REPLICA),
        ),
        out_specs=(P(REPLICA, FSDP, None), P(FSDP), P(FSDP + REPLICA)),
        check_vma=False,
    )
```

```python
import functools

import jax
import jax.numpy as jnp
from jax import lax
from jax.experimental import pallas as pl
from jax.experimental.pallas import tpu as pltpu
from jax.sharding import Mesh
from jax.sharding import PartitionSpec as P

QBLOCK = 128
LANES = 128


outer_decay = 0.9
outer_rate = 0.7
clip_ratio = 2.0
epsilon = 1e-06

AXES = {"z": 8, "y_lo": 2, "y_hi": 4, "x": 4, "core": 2}
REPLICA = ("z", "y_lo")
FSDP = ("y_hi", "x", "core")
CHIPS = AXES["x"] * AXES["y_hi"]
STEPS = (2, 1, 3)


def encode(difference):
    blocks = difference.reshape(-1, QBLOCK)
    scales = (clip_ratio * jnp.sqrt(jnp.mean(blocks * blocks, axis=-1) + epsilon)).astype(
        jnp.bfloat16
    )
    block_codes = jnp.clip(blocks / scales.astype(jnp.float32)[:, None], -1.0, 1.0).astype(
        jnp.bfloat16
    )
    return (block_codes, scales)


def send(value, axis, step):
    size = AXES[axis]
    return lax.ppermute(value, axis, [(i, (i + step) % size) for i in range(size)])


def tied(*values):
    return lax.optimization_barrier(values)


def arrange_kernel(order_ref, inputs_ref, theirs_ref, gain_ref, scaled_ref):
    tokens = inputs_ref.shape[0]
    for j in range(CHIPS):
        start = pl.multiple_of(order_ref[j] * LANES, LANES)
        columns = pl.ds(start, LANES)
        place = slice(j * LANES, (j + 1) * LANES)
        for row, ref in ((0, inputs_ref), (tokens, theirs_ref)):
            scaled_ref[row : row + tokens, place] = (
                ref[:, columns].astype(jnp.float32) * gain_ref[:, columns]
            ).astype(jnp.bfloat16)


def arrange(inputs, theirs, feature_gain):
    tokens, features = inputs.shape
    x, y, core = (lax.axis_index(name) for name in ("x", "y_hi", "core"))
    rx, ry = jnp.arange(CHIPS) // AXES["y_hi"], jnp.arange(CHIPS) % AXES["y_hi"]
    chip = (y + ry) % AXES["y_hi"] * AXES["x"] + (x + rx) % AXES["x"]
    order = (chip * 2 + core).astype(jnp.int32)
    in_vmem = pl.BlockSpec(memory_space=pltpu.VMEM)
    return pl.pallas_call(
        arrange_kernel,
        out_shape=jax.ShapeDtypeStruct((2 * tokens, features // 2), jnp.bfloat16),
        in_specs=[pl.BlockSpec(memory_space=pltpu.SMEM)] + [in_vmem] * 3,
        out_specs=in_vmem,
        compiler_params=pltpu.CompilerParams(vmem_limit_bytes=24 << 20),
        name="arrange",
    )(order, inputs, theirs, feature_gain[None, :])


def exchange(parts, axis):
    return lax.all_to_all(parts, axis, split_axis=0, concat_axis=0, tiled=True)


def spread(value, axis):
    return exchange(jnp.broadcast_to(value[None], (lax.axis_size(axis), *value.shape)), axis)


def total(values):
    return functools.reduce(jnp.add, [value.astype(jnp.float32) for value in values])


def fragment_codes(global_frag, local_frag):
    difference = global_frag.astype(jnp.float32) - local_frag.astype(jnp.float32)
    block_codes, scales = encode(difference)
    decoded = block_codes.astype(jnp.float32) * scales.astype(jnp.float32)[:, None]
    return decoded.astype(jnp.bfloat16).reshape(lax.axis_size(REPLICA), -1, QBLOCK)


def fragment_update(arrived, global_frag, momentum):
    replicas, rows = arrived.shape[:2]
    share = rows * QBLOCK
    pseudo = jnp.sum(arrived.astype(jnp.float32), axis=0) / replicas
    new_momentum = outer_decay * momentum.reshape(rows, QBLOCK) + pseudo
    offset = lax.axis_index(REPLICA) * share
    own_global = lax.dynamic_slice_in_dim(global_frag, offset, share).reshape(rows, QBLOCK)
    own_next = (
        own_global.astype(jnp.float32) - outer_rate * (pseudo + outer_decay * new_momentum)
    ).astype(jnp.bfloat16)
    return spread(own_next, REPLICA).reshape(-1), new_momentum.reshape(-1)


def shards(inputs, feature_gain, key_weight, teacher_keys, global_frag, local_frag, momentum):
    tokens, features = inputs.shape[1:]
    rows, width = key_weight.shape[1:]

    weight = key_weight[0]
    near = [weight] + [None] * 3
    for k in STEPS:
        near[k] = send(weight, "y_hi", -k)
    raw = send(inputs[0], "core", 1)
    targets = [teacher_keys[0], send(teacher_keys[0], "core", 1)]
    column = jnp.concatenate(near, axis=0)
    column, global_frag, local_frag = tied(column, global_frag, local_frag)
    far = {k: send(column, "x", -k) for k in STEPS}
    arrived = exchange(fragment_codes(global_frag, local_frag[0]), REPLICA)
    scaled = arrange(inputs[0], raw, feature_gain)
    group = scaled.shape[1] // AXES["x"]
    blocks = [scaled[:, k * group : (k + 1) * group] for k in range(AXES["x"])]
    partial = jnp.dot(blocks[0], column, preferred_element_type=jnp.float32)
    for k in STEPS:
        if k == STEPS[-1]:
            partial, arrived, targets = tied(partial, arrived, targets)
        partial += jnp.dot(blocks[k], far[k], preferred_element_type=jnp.float32)

    theirs = send(partial, "core", 1)
    residual = [
        (mine + other - target.astype(jnp.float32)).astype(jnp.bfloat16)
        for mine, other, target in zip(
            (partial[:tokens], partial[tokens:]), (theirs[tokens:], theirs[:tokens]), targets
        )
    ]
    residual = jnp.concatenate(residual, axis=0)
    gradient = [
        lax.dot_general(
            block, residual, (((0,), (0,)), ((), ())), preferred_element_type=jnp.float32
        ).astype(jnp.bfloat16)
        for block in blocks
    ]
    gradient[0], arrived = tied(gradient[0], arrived)
    new_global, new_momentum = fragment_update(arrived, global_frag, momentum)
    arrivals = [send(gradient[k], "x", k) for k in STEPS]
    arrivals, new_global = tied(arrivals, new_global)
    mine = total([gradient[0]] + arrivals)
    mine = mine.astype(jnp.bfloat16).reshape(AXES["y_hi"], rows, width)
    gradient = total([mine[0]] + [send(mine[k], "y_hi", k) for k in STEPS])

    squares = jnp.sum(gradient * gradient)
    mean_square = jnp.sum(spread(squares[None], FSDP)) / (features * width)
    factor = jnp.minimum(1.0, lax.rsqrt(mean_square + epsilon))
    clipped_grad = (gradient * factor).astype(jnp.bfloat16)[None]
    return (clipped_grad, new_global, new_momentum)


def solution(mesh):
    parted = Mesh(mesh.devices.reshape(tuple(AXES.values())), tuple(AXES))
    return jax.shard_map(
        shards,
        mesh=parted,
        in_specs=(
            P(REPLICA, FSDP, None),
            P(),
            P(REPLICA, FSDP, None),
            P(REPLICA, FSDP, None),
            P(FSDP),
            P(REPLICA, FSDP),
            P(FSDP + REPLICA),
        ),
        out_specs=(P(REPLICA, FSDP, None), P(FSDP), P(FSDP + REPLICA)),
        check_vma=False,
    )
```

```python
import functools

import jax
import jax.numpy as jnp
from jax import lax
from jax.experimental import pallas as pl
from jax.experimental.pallas import tpu as pltpu
from jax.sharding import Mesh
from jax.sharding import PartitionSpec as P

QBLOCK = 128
LANES = 128


outer_decay = 0.9
outer_rate = 0.7
clip_ratio = 2.0
epsilon = 1e-06

AXES = {"z": 8, "y_lo": 2, "y_hi": 4, "x": 4, "core": 2}
REPLICA = ("z", "y_lo")
FSDP = ("y_hi", "x", "core")
CHIPS = AXES["x"] * AXES["y_hi"]
STEPS = (2, 1, 3)


def encode(difference):
    blocks = difference.reshape(-1, QBLOCK)
    scales = (clip_ratio * jnp.sqrt(jnp.mean(blocks * blocks, axis=-1) + epsilon)).astype(
        jnp.bfloat16
    )
    block_codes = jnp.clip(blocks / scales.astype(jnp.float32)[:, None], -1.0, 1.0).astype(
        jnp.bfloat16
    )
    return (block_codes, scales)


def send(value, axis, step):
    size = AXES[axis]
    return lax.ppermute(value, axis, [(i, (i + step) % size) for i in range(size)])


def tied(*values):
    return lax.optimization_barrier(values)


def arrange_kernel(order_ref, inputs_ref, theirs_ref, gain_ref, scaled_ref):
    for j in range(CHIPS):
        start = pl.multiple_of(order_ref[j] * LANES, LANES)
        columns = pl.ds(start, LANES)
        gain = gain_ref[:, columns]
        for half, ref in enumerate((inputs_ref, theirs_ref)):
            scaled_ref[half, :, j * LANES : (j + 1) * LANES] = (
                ref[:, columns].astype(jnp.float32) * gain
            ).astype(jnp.bfloat16)


def arrange(inputs, theirs, feature_gain):
    tokens, features = inputs.shape
    x, y, core = (lax.axis_index(name) for name in ("x", "y_hi", "core"))
    rx, ry = jnp.arange(CHIPS) // AXES["y_hi"], jnp.arange(CHIPS) % AXES["y_hi"]
    chip = (y + ry) % AXES["y_hi"] * AXES["x"] + (x + rx) % AXES["x"]
    order = (chip * 2 + core).astype(jnp.int32)
    step = 96
    block = pl.BlockSpec((step, features), lambda i: (i, 0))
    scaled = pl.pallas_call(
        arrange_kernel,
        grid=(tokens // step,),
        out_shape=jax.ShapeDtypeStruct((2, tokens, features // 2), jnp.bfloat16),
        in_specs=[
            pl.BlockSpec(memory_space=pltpu.SMEM),
            block,
            block,
            pl.BlockSpec((1, features), lambda i: (0, 0)),
        ],
        out_specs=pl.BlockSpec((2, step, features // 2), lambda i: (0, i, 0)),
        compiler_params=pltpu.CompilerParams(vmem_limit_bytes=24 << 20),
        name="arrange",
    )(order, inputs, theirs, feature_gain[None, :])
    return scaled.reshape(2 * tokens, features // 2)


def exchange(parts, axis):
    return lax.all_to_all(parts, axis, split_axis=0, concat_axis=0, tiled=True)


def spread(value, axis):
    return exchange(jnp.broadcast_to(value[None], (lax.axis_size(axis), *value.shape)), axis)


def total(values):
    return functools.reduce(jnp.add, [value.astype(jnp.float32) for value in values])


def fragment_codes(global_frag, local_frag):
    difference = global_frag.astype(jnp.float32) - local_frag.astype(jnp.float32)
    block_codes, scales = encode(difference)
    decoded = block_codes.astype(jnp.float32) * scales.astype(jnp.float32)[:, None]
    return decoded.astype(jnp.bfloat16).reshape(lax.axis_size(REPLICA), -1, QBLOCK)


def fragment_update(arrived, global_frag, momentum):
    replicas, rows = arrived.shape[:2]
    share = rows * QBLOCK
    pseudo = jnp.sum(arrived.astype(jnp.float32), axis=0) / replicas
    new_momentum = outer_decay * momentum.reshape(rows, QBLOCK) + pseudo
    offset = lax.axis_index(REPLICA) * share
    own_global = lax.dynamic_slice_in_dim(global_frag, offset, share).reshape(rows, QBLOCK)
    own_next = (
        own_global.astype(jnp.float32) - outer_rate * (pseudo + outer_decay * new_momentum)
    ).astype(jnp.bfloat16)
    return spread(own_next, REPLICA).reshape(-1), new_momentum.reshape(-1)


def shards(inputs, feature_gain, key_weight, teacher_keys, global_frag, local_frag, momentum):
    tokens, features = inputs.shape[1:]
    rows, width = key_weight.shape[1:]

    weight = key_weight[0]
    near = [weight] + [None] * 3
    for k in STEPS:
        near[k] = send(weight, "y_hi", -k)
    near[1], inputs, teacher_keys, global_frag, local_frag = tied(
        near[1], inputs, teacher_keys, global_frag, local_frag
    )
    raw = send(inputs[0], "core", 1)
    their_targets = send(teacher_keys[0], "core", 1)
    arrived = exchange(fragment_codes(global_frag, local_frag[0]), REPLICA)
    column = jnp.concatenate(near, axis=0)
    far = {k: send(column, "x", -k) for k in STEPS}
    new_global, new_momentum = fragment_update(arrived, global_frag, momentum)
    targets = jnp.concatenate([teacher_keys[0], their_targets], axis=0)
    scaled = arrange(inputs[0], raw, feature_gain)
    group = scaled.shape[1] // AXES["x"]
    blocks = [scaled[:, k * group : (k + 1) * group] for k in range(AXES["x"])]
    partial = jnp.dot(blocks[0], column, preferred_element_type=jnp.float32)
    last = STEPS[-1]
    far[last], new_global, targets = tied(far[last], new_global, targets)
    for k in STEPS:
        partial += jnp.dot(blocks[k], far[k], preferred_element_type=jnp.float32)

    theirs = send(partial, "core", 1)
    projected = partial + jnp.concatenate([theirs[tokens:], theirs[:tokens]], axis=0)
    residual = (projected - targets.astype(jnp.float32)).astype(jnp.bfloat16)
    gradient = [
        lax.dot_general(
            block, residual, (((0,), (0,)), ((), ())), preferred_element_type=jnp.float32
        ).astype(jnp.bfloat16)
        for block in blocks
    ]
    mine = total([gradient[0]] + [send(gradient[k], "x", k) for k in STEPS])
    mine = mine.astype(jnp.bfloat16).reshape(AXES["y_hi"], rows, width)
    gradient = total([mine[0]] + [send(mine[k], "y_hi", k) for k in STEPS])

    squares = jnp.sum(gradient * gradient)
    mean_square = jnp.sum(spread(squares[None], FSDP)) / (features * width)
    factor = jnp.minimum(1.0, lax.rsqrt(mean_square + epsilon))
    clipped_grad = (gradient * factor).astype(jnp.bfloat16)[None]
    return (clipped_grad, new_global, new_momentum)


def solution(mesh):
    parted = Mesh(mesh.devices.reshape(tuple(AXES.values())), tuple(AXES))
    return jax.shard_map(
        shards,
        mesh=parted,
        in_specs=(
            P(REPLICA, FSDP, None),
            P(),
            P(REPLICA, FSDP, None),
            P(REPLICA, FSDP, None),
            P(FSDP),
            P(REPLICA, FSDP),
            P(FSDP + REPLICA),
        ),
        out_specs=(P(REPLICA, FSDP, None), P(FSDP), P(FSDP + REPLICA)),
        check_vma=False,
    )
```

```python
import functools

import jax
import jax.numpy as jnp
from jax import lax
from jax.experimental import pallas as pl
from jax.experimental.pallas import tpu as pltpu
from jax.sharding import Mesh
from jax.sharding import PartitionSpec as P

QBLOCK = 128
LANES = 128


outer_decay = 0.9
outer_rate = 0.7
clip_ratio = 2.0
epsilon = 1e-06

AXES = {"z": 8, "y_lo": 2, "y_hi": 4, "x": 4, "core": 2}
REPLICA = ("z", "y_lo")
FSDP = ("y_hi", "x", "core")
CHIPS = AXES["x"] * AXES["y_hi"]
STEPS = (2, 1, 3)


def encode(difference):
    blocks = difference.reshape(-1, QBLOCK)
    scales = (clip_ratio * jnp.sqrt(jnp.mean(blocks * blocks, axis=-1) + epsilon)).astype(
        jnp.bfloat16
    )
    block_codes = jnp.clip(blocks / scales.astype(jnp.float32)[:, None], -1.0, 1.0).astype(
        jnp.bfloat16
    )
    return (block_codes, scales)


def send(value, axis, step):
    size = AXES[axis]
    return lax.ppermute(value, axis, [(i, (i + step) % size) for i in range(size)])


def tied(*values):
    return lax.optimization_barrier(values)


def arrange_kernel(order_ref, inputs_ref, theirs_ref, gain_ref, scaled_ref):
    for j in range(CHIPS):
        start = pl.multiple_of(order_ref[j] * LANES, LANES)
        columns = pl.ds(start, LANES)
        gain = gain_ref[:, columns]
        for half, ref in enumerate((inputs_ref, theirs_ref)):
            scaled_ref[half, :, j * LANES : (j + 1) * LANES] = (
                ref[:, columns].astype(jnp.float32) * gain
            ).astype(jnp.bfloat16)


def arrange(inputs, theirs, feature_gain):
    tokens, features = inputs.shape
    x, core = lax.axis_index("x"), lax.axis_index("core")
    rx, y = jnp.arange(CHIPS) // AXES["y_hi"], jnp.arange(CHIPS) % AXES["y_hi"]
    chip = y * AXES["x"] + (x + rx) % AXES["x"]
    order = (chip * 2 + core).astype(jnp.int32)
    step = 96
    block = pl.BlockSpec((step, features), lambda i: (i, 0))
    scaled = pl.pallas_call(
        arrange_kernel,
        grid=(tokens // step,),
        out_shape=jax.ShapeDtypeStruct((2, tokens, features // 2), jnp.bfloat16),
        in_specs=[
            pl.BlockSpec(memory_space=pltpu.SMEM),
            block,
            block,
            pl.BlockSpec((1, features), lambda i: (0, 0)),
        ],
        out_specs=pl.BlockSpec((2, step, features // 2), lambda i: (0, i, 0)),
        compiler_params=pltpu.CompilerParams(vmem_limit_bytes=24 << 20),
        name="arrange",
    )(order, inputs, theirs, feature_gain[None, :])
    return scaled.reshape(2 * tokens, features // 2)


def exchange(parts, axis):
    return lax.all_to_all(parts, axis, split_axis=0, concat_axis=0, tiled=True)


def spread(value, axis):
    return exchange(jnp.broadcast_to(value[None], (lax.axis_size(axis), *value.shape)), axis)


def total(values):
    return functools.reduce(jnp.add, [value.astype(jnp.float32) for value in values])


def fragment_codes(global_frag, local_frag):
    difference = global_frag.astype(jnp.float32) - local_frag.astype(jnp.float32)
    block_codes, scales = encode(difference)
    decoded = block_codes.astype(jnp.float32) * scales.astype(jnp.float32)[:, None]
    return decoded.astype(jnp.bfloat16).reshape(lax.axis_size(REPLICA), -1, QBLOCK)


def fragment_update(arrived, global_frag, momentum):
    replicas, rows = arrived.shape[:2]
    share = rows * QBLOCK
    pseudo = jnp.sum(arrived.astype(jnp.float32), axis=0) / replicas
    new_momentum = outer_decay * momentum.reshape(rows, QBLOCK) + pseudo
    offset = lax.axis_index(REPLICA) * share
    own_global = lax.dynamic_slice_in_dim(global_frag, offset, share).reshape(rows, QBLOCK)
    own_next = (
        own_global.astype(jnp.float32) - outer_rate * (pseudo + outer_decay * new_momentum)
    ).astype(jnp.bfloat16)
    return spread(own_next, REPLICA).reshape(-1), new_momentum.reshape(-1)


def collect_kernel(arrived_ref, gradient_ref, squares_ref):
    gradient = total([arrived_ref[k] for k in range(arrived_ref.shape[0])])
    gradient_ref[...] = gradient
    squares = jnp.sum(gradient * gradient, axis=0, keepdims=True)
    squares_ref[...] = jnp.broadcast_to(
        jnp.sum(squares, axis=1, keepdims=True), squares_ref.shape
    )


def collect(arrived):
    in_vmem = pl.BlockSpec(memory_space=pltpu.VMEM)
    return pl.pallas_call(
        collect_kernel,
        out_shape=(
            jax.ShapeDtypeStruct(arrived.shape[1:], jnp.float32),
            jax.ShapeDtypeStruct((CHIPS * AXES["core"], LANES), jnp.float32),
        ),
        in_specs=[in_vmem],
        out_specs=(in_vmem, in_vmem),
        name="collect",
    )(arrived)


def clip_kernel(entries, squares_ref, gradient_ref, clipped_ref):
    mean_square = jnp.sum(squares_ref[...], axis=0, keepdims=True) / entries
    factor = jnp.minimum(1.0, lax.rsqrt(mean_square + epsilon))
    for j in range(gradient_ref.shape[1] // LANES):
        columns = slice(j * LANES, (j + 1) * LANES)
        clipped_ref[:, columns] = (gradient_ref[:, columns] * factor).astype(jnp.bfloat16)


def clip(squares, gradient, entries):
    in_vmem = pl.BlockSpec(memory_space=pltpu.VMEM)
    return pl.pallas_call(
        functools.partial(clip_kernel, entries),
        out_shape=jax.ShapeDtypeStruct(gradient.shape, jnp.bfloat16),
        in_specs=[in_vmem, in_vmem],
        out_specs=in_vmem,
        name="clip",
    )(squares, gradient)


def shards(inputs, feature_gain, key_weight, teacher_keys, global_frag, local_frag, momentum):
    tokens, features = inputs.shape[1:]
    rows, width = key_weight.shape[1:]

    column = spread(key_weight[0], "y_hi").reshape(AXES["y_hi"] * rows, width)
    raw = send(inputs[0], "core", 1)
    their_targets = send(teacher_keys[0], "core", 1)
    decoded = fragment_codes(global_frag, local_frag[0])
    column, decoded = tied(column, decoded)
    far = {k: send(column, "x", -k) for k in STEPS}
    arrived = exchange(decoded, REPLICA)
    targets = jnp.concatenate([teacher_keys[0], their_targets], axis=0)
    scaled = arrange(inputs[0], raw, feature_gain)
    group = scaled.shape[1] // AXES["x"]
    blocks = [scaled[:, k * group : (k + 1) * group] for k in range(AXES["x"])]
    partial = jnp.dot(blocks[0], column, preferred_element_type=jnp.float32)
    last = STEPS[-1]
    far[last], arrived, targets = tied(far[last], arrived, targets)
    for k in STEPS:
        partial += jnp.dot(blocks[k], far[k], preferred_element_type=jnp.float32)

    theirs = send(partial, "core", 1)
    projected = partial + jnp.concatenate([theirs[tokens:], theirs[:tokens]], axis=0)
    residual = (projected - targets.astype(jnp.float32)).astype(jnp.bfloat16)
    gradient = [
        lax.dot_general(
            block, residual, (((0,), (0,)), ((), ())), preferred_element_type=jnp.float32
        ).astype(jnp.bfloat16)
        for block in blocks
    ]
    gradient[0], arrived = tied(gradient[0], arrived)
    new_global, new_momentum = fragment_update(arrived, global_frag, momentum)
    mine = total([gradient[0]] + [send(gradient[k], "x", k) for k in STEPS])
    mine, new_global = tied(mine.astype(jnp.bfloat16), new_global)
    gradient, squares = collect(exchange(mine.reshape(AXES["y_hi"], rows, width), "y_hi"))

    clipped_grad = clip(exchange(squares, FSDP), gradient, features * width)[None]
    return (clipped_grad, new_global, new_momentum)


def solution(mesh):
    parted = Mesh(mesh.devices.reshape(tuple(AXES.values())), tuple(AXES))
    return jax.shard_map(
        shards,
        mesh=parted,
        in_specs=(
            P(REPLICA, FSDP, None),
            P(),
            P(REPLICA, FSDP, None),
            P(REPLICA, FSDP, None),
            P(FSDP),
            P(REPLICA, FSDP),
            P(FSDP + REPLICA),
        ),
        out_specs=(P(REPLICA, FSDP, None), P(FSDP), P(FSDP + REPLICA)),
        check_vma=False,
    )
```

```python
import functools

import jax
import jax.numpy as jnp
from jax import lax
from jax.experimental import pallas as pl
from jax.experimental.pallas import tpu as pltpu
from jax.sharding import Mesh
from jax.sharding import PartitionSpec as P

QBLOCK = 128
LANES = 128
VMEM_LIMIT = 8 << 20


outer_decay = 0.9
outer_rate = 0.7
clip_ratio = 2.0
epsilon = 1e-06

AXES = {"z": 8, "y_lo": 2, "y_hi": 4, "x": 4, "core": 2}
REPLICA = ("z", "y_lo")
FSDP = ("y_hi", "x", "core")
CHIPS = AXES["x"] * AXES["y_hi"]
STEPS = (2, 1, 3)


def encode(difference):
    blocks = difference.reshape(-1, QBLOCK)
    scales = (clip_ratio * jnp.sqrt(jnp.mean(blocks * blocks, axis=-1) + epsilon)).astype(
        jnp.bfloat16
    )
    block_codes = jnp.clip(blocks / scales.astype(jnp.float32)[:, None], -1.0, 1.0).astype(
        jnp.bfloat16
    )
    return (block_codes, scales)


def send(value, axis, step):
    size = AXES[axis]
    return lax.ppermute(value, axis, [(i, (i + step) % size) for i in range(size)])


def tied(*values):
    return lax.optimization_barrier(values)


def arrange_kernel(order_ref, inputs_ref, theirs_ref, gain_ref, scaled_ref):
    for j in range(CHIPS):
        start = pl.multiple_of(order_ref[j] * LANES, LANES)
        columns = pl.ds(start, LANES)
        gain = gain_ref[:, columns]
        for half, ref in enumerate((inputs_ref, theirs_ref)):
            scaled_ref[half, :, j * LANES : (j + 1) * LANES] = (
                ref[:, columns].astype(jnp.float32) * gain
            ).astype(jnp.bfloat16)


def arrange(inputs, theirs, feature_gain):
    tokens, features = inputs.shape
    x, core = lax.axis_index("x"), lax.axis_index("core")
    rx, y = jnp.arange(CHIPS) // AXES["y_hi"], jnp.arange(CHIPS) % AXES["y_hi"]
    chip = y * AXES["x"] + (x + rx) % AXES["x"]
    order = (chip * 2 + core).astype(jnp.int32)
    step = 32
    block = pl.BlockSpec((step, features), lambda i: (i, 0))
    scaled = pl.pallas_call(
        arrange_kernel,
        grid=(tokens // step,),
        out_shape=jax.ShapeDtypeStruct((2, tokens, features // 2), jnp.bfloat16),
        in_specs=[
            pl.BlockSpec(memory_space=pltpu.SMEM),
            block,
            block,
            pl.BlockSpec((1, features), lambda i: (0, 0)),
        ],
        out_specs=pl.BlockSpec((2, step, features // 2), lambda i: (0, i, 0)),
        compiler_params=pltpu.CompilerParams(vmem_limit_bytes=VMEM_LIMIT),
        name="arrange",
    )(order, inputs, theirs, feature_gain[None, :])
    return scaled.reshape(2 * tokens, features // 2)


def exchange(parts, axis):
    return lax.all_to_all(parts, axis, split_axis=0, concat_axis=0, tiled=True)


def spread(value, axis):
    return exchange(jnp.broadcast_to(value[None], (lax.axis_size(axis), *value.shape)), axis)


def total(values):
    return functools.reduce(jnp.add, [value.astype(jnp.float32) for value in values])


def fragment_codes(global_frag, local_frag):
    difference = global_frag.astype(jnp.float32) - local_frag.astype(jnp.float32)
    block_codes, scales = encode(difference)
    decoded = block_codes.astype(jnp.float32) * scales.astype(jnp.float32)[:, None]
    return decoded.astype(jnp.bfloat16).reshape(lax.axis_size(REPLICA), -1, QBLOCK)


def fragment_update(arrived, global_frag, momentum):
    replicas, rows = arrived.shape[:2]
    share = rows * QBLOCK
    pseudo = jnp.sum(arrived.astype(jnp.float32), axis=0) / replicas
    new_momentum = outer_decay * momentum.reshape(rows, QBLOCK) + pseudo
    offset = lax.axis_index(REPLICA) * share
    own_global = lax.dynamic_slice_in_dim(global_frag, offset, share).reshape(rows, QBLOCK)
    own_next = (
        own_global.astype(jnp.float32) - outer_rate * (pseudo + outer_decay * new_momentum)
    ).astype(jnp.bfloat16)
    return spread(own_next, REPLICA).reshape(-1), new_momentum.reshape(-1)


def collect_kernel(arrived_ref, gradient_ref, squares_ref):
    gradient = total([arrived_ref[k] for k in range(arrived_ref.shape[0])])
    gradient_ref[...] = gradient
    squares = jnp.sum(gradient * gradient, axis=0, keepdims=True)
    squares_ref[...] = jnp.broadcast_to(
        jnp.sum(squares, axis=1, keepdims=True), squares_ref.shape
    )


def collect(arrived):
    in_vmem = pl.BlockSpec(memory_space=pltpu.VMEM)
    return pl.pallas_call(
        collect_kernel,
        out_shape=(
            jax.ShapeDtypeStruct(arrived.shape[1:], jnp.float32),
            jax.ShapeDtypeStruct((CHIPS * AXES["core"], LANES), jnp.float32),
        ),
        in_specs=[in_vmem],
        out_specs=(in_vmem, in_vmem),
        compiler_params=pltpu.CompilerParams(vmem_limit_bytes=VMEM_LIMIT),
        name="collect",
    )(arrived)


def clip_kernel(entries, squares_ref, gradient_ref, clipped_ref):
    mean_square = jnp.sum(squares_ref[...], axis=0, keepdims=True) / entries
    factor = jnp.minimum(1.0, lax.rsqrt(mean_square + epsilon))
    for j in range(gradient_ref.shape[1] // LANES):
        columns = slice(j * LANES, (j + 1) * LANES)
        clipped_ref[:, columns] = (gradient_ref[:, columns] * factor).astype(jnp.bfloat16)


def clip(squares, gradient, entries):
    in_vmem = pl.BlockSpec(memory_space=pltpu.VMEM)
    return pl.pallas_call(
        functools.partial(clip_kernel, entries),
        out_shape=jax.ShapeDtypeStruct(gradient.shape, jnp.bfloat16),
        in_specs=[in_vmem, in_vmem],
        out_specs=in_vmem,
        compiler_params=pltpu.CompilerParams(vmem_limit_bytes=VMEM_LIMIT),
        name="clip",
    )(squares, gradient)


def shards(inputs, feature_gain, key_weight, teacher_keys, global_frag, local_frag, momentum):
    tokens, features = inputs.shape[1:]
    rows, width = key_weight.shape[1:]

    column = spread(key_weight[0], "y_hi").reshape(AXES["y_hi"] * rows, width)
    raw = send(inputs[0], "core", 1)
    their_targets = send(teacher_keys[0], "core", 1)
    targets = jnp.concatenate([teacher_keys[0], their_targets], axis=0)
    scaled = arrange(inputs[0], raw, feature_gain)
    column, scaled, targets, global_frag, local_frag = tied(
        column, scaled, targets, global_frag, local_frag
    )
    far = {k: send(column, "x", -k) for k in STEPS}
    arrived = exchange(fragment_codes(global_frag, local_frag[0]), REPLICA)
    group = scaled.shape[1] // AXES["x"]
    blocks = [scaled[:, k * group : (k + 1) * group] for k in range(AXES["x"])]
    partial = jnp.dot(blocks[0], column, preferred_element_type=jnp.float32)
    last = STEPS[-1]
    far[last], arrived = tied(far[last], arrived)
    for k in STEPS:
        partial += jnp.dot(blocks[k], far[k], preferred_element_type=jnp.float32)

    theirs = send(partial, "core", 1)
    projected = partial + jnp.concatenate([theirs[tokens:], theirs[:tokens]], axis=0)
    residual = (projected - targets.astype(jnp.float32)).astype(jnp.bfloat16)
    gradient = [
        lax.dot_general(
            block, residual, (((0,), (0,)), ((), ())), preferred_element_type=jnp.float32
        ).astype(jnp.bfloat16)
        for block in blocks
    ]
    gradient[0], arrived = tied(gradient[0], arrived)
    new_global, new_momentum = fragment_update(arrived, global_frag, momentum)
    mine = total([gradient[0]] + [send(gradient[k], "x", k) for k in STEPS])
    mine, new_global = tied(mine.astype(jnp.bfloat16), new_global)
    gradient, squares = collect(exchange(mine.reshape(AXES["y_hi"], rows, width), "y_hi"))

    clipped_grad = clip(exchange(squares, FSDP), gradient, features * width)[None]
    return (clipped_grad, new_global, new_momentum)


def solution(mesh):
    parted = Mesh(mesh.devices.reshape(tuple(AXES.values())), tuple(AXES))
    return jax.shard_map(
        shards,
        mesh=parted,
        in_specs=(
            P(REPLICA, FSDP, None),
            P(),
            P(REPLICA, FSDP, None),
            P(REPLICA, FSDP, None),
            P(FSDP),
            P(REPLICA, FSDP),
            P(FSDP + REPLICA),
        ),
        out_specs=(P(REPLICA, FSDP, None), P(FSDP), P(FSDP + REPLICA)),
        check_vma=False,
    )
```

```python
import functools

import jax
import jax.numpy as jnp
from jax import lax
from jax.experimental import pallas as pl
from jax.experimental.pallas import tpu as pltpu
from jax.sharding import Mesh
from jax.sharding import PartitionSpec as P

QBLOCK = 128
LANES = 128
VMEM_LIMIT = 8 << 20
WHOLE = pl.BlockSpec(memory_space=pltpu.VMEM)


outer_decay = 0.9
outer_rate = 0.7
clip_ratio = 2.0
epsilon = 1e-06

AXES = {"z": 8, "y_lo": 2, "y_hi": 4, "x": 4, "core": 2}
REPLICA = ("z", "y_lo")
FSDP = ("y_hi", "x", "core")
CHIPS = AXES["x"] * AXES["y_hi"]
STEPS = (2, 1, 3)


def encode(difference):
    blocks = difference.reshape(-1, QBLOCK)
    scales = (clip_ratio * jnp.sqrt(jnp.mean(blocks * blocks, axis=-1) + epsilon)).astype(
        jnp.bfloat16
    )
    block_codes = jnp.clip(blocks / scales.astype(jnp.float32)[:, None], -1.0, 1.0).astype(
        jnp.bfloat16
    )
    return (block_codes, scales)


def send(value, axis, step):
    size = AXES[axis]
    return lax.ppermute(value, axis, [(i, (i + step) % size) for i in range(size)])


def tied(*values):
    return lax.optimization_barrier(values)


def arrange_kernel(order_ref, inputs_ref, theirs_ref, gain_ref, scaled_ref):
    for j in range(CHIPS):
        start = pl.multiple_of(order_ref[j] * LANES, LANES)
        columns = pl.ds(start, LANES)
        gain = gain_ref[:, columns]
        for half, ref in enumerate((inputs_ref, theirs_ref)):
            scaled_ref[half, :, j * LANES : (j + 1) * LANES] = (
                ref[:, columns].astype(jnp.float32) * gain
            ).astype(jnp.bfloat16)


def arrange(inputs, theirs, feature_gain):
    tokens, features = inputs.shape
    x, core = lax.axis_index("x"), lax.axis_index("core")
    rx, y = jnp.arange(CHIPS) // AXES["y_hi"], jnp.arange(CHIPS) % AXES["y_hi"]
    chip = y * AXES["x"] + (x + rx) % AXES["x"]
    order = (chip * 2 + core).astype(jnp.int32)
    step = 32
    block = pl.BlockSpec((step, features), lambda i: (i, 0))
    scaled = pl.pallas_call(
        arrange_kernel,
        grid=(tokens // step,),
        out_shape=jax.ShapeDtypeStruct((2, tokens, features // 2), jnp.bfloat16),
        in_specs=[
            pl.BlockSpec(memory_space=pltpu.SMEM),
            block,
            block,
            pl.BlockSpec((1, features), lambda i: (0, 0)),
        ],
        out_specs=pl.BlockSpec((2, step, features // 2), lambda i: (0, i, 0)),
        compiler_params=pltpu.CompilerParams(vmem_limit_bytes=VMEM_LIMIT),
        name="arrange",
    )(order, inputs, theirs, feature_gain[None, :])
    return scaled.reshape(2 * tokens, features // 2)


def exchange(parts, axis):
    return lax.all_to_all(parts, axis, split_axis=0, concat_axis=0, tiled=True)


def spread(value, axis):
    return exchange(jnp.broadcast_to(value[None], (lax.axis_size(axis), *value.shape)), axis)


def total(values):
    return functools.reduce(jnp.add, [value.astype(jnp.float32) for value in values])


def fragment_codes(global_frag, local_frag):
    difference = global_frag.astype(jnp.float32) - local_frag.astype(jnp.float32)
    block_codes, scales = encode(difference)
    decoded = block_codes.astype(jnp.float32) * scales.astype(jnp.float32)[:, None]
    return decoded.astype(jnp.bfloat16).reshape(lax.axis_size(REPLICA), -1, QBLOCK)


def fragment_update(arrived, global_frag, momentum):
    replicas, rows = arrived.shape[:2]
    share = rows * QBLOCK
    pseudo = jnp.sum(arrived.astype(jnp.float32), axis=0) / replicas
    new_momentum = outer_decay * momentum.reshape(rows, QBLOCK) + pseudo
    offset = lax.axis_index(REPLICA) * share
    own_global = lax.dynamic_slice_in_dim(global_frag, offset, share).reshape(rows, QBLOCK)
    own_next = (
        own_global.astype(jnp.float32) - outer_rate * (pseudo + outer_decay * new_momentum)
    ).astype(jnp.bfloat16)
    return spread(own_next, REPLICA).reshape(-1), new_momentum.reshape(-1)


def in_vmem(shape, dtype):
    return pltpu.VMEM(shape, dtype)


def product_kernel(scaled_ref, *refs):
    *weight_refs, partial_ref = refs
    group = weight_refs[0].shape[0]
    partial_ref[...] = total(
        [
            jnp.dot(
                scaled_ref[:, k * group : (k + 1) * group],
                ref[...],
                preferred_element_type=jnp.float32,
            )
            for k, ref in enumerate(weight_refs)
        ]
    )


def product(scaled, weights):
    return pl.pallas_call(
        product_kernel,
        out_shape=in_vmem((scaled.shape[0], weights[0].shape[1]), jnp.float32),
        in_specs=[WHOLE] * (1 + len(weights)),
        out_specs=WHOLE,
        compiler_params=pltpu.CompilerParams(vmem_limit_bytes=2 * VMEM_LIMIT),
        name="product",
    )(scaled, *weights)


def gradient_kernel(scaled_ref, mine_ref, theirs_ref, *refs):
    *target_refs, first, second, third, fourth, residual_ref = refs
    tokens = target_refs[0].shape[0]
    for half, target_ref in enumerate(target_refs):
        here = slice(half * tokens, (half + 1) * tokens)
        there = slice((1 - half) * tokens, (2 - half) * tokens)
        residual_ref[here, :] = (
            mine_ref[here, :] + theirs_ref[there, :] - target_ref[...].astype(jnp.float32)
        ).astype(jnp.bfloat16)
    group = first.shape[0]
    for k, ref in enumerate((first, second, third, fourth)):
        ref[...] = lax.dot_general(
            scaled_ref[:, k * group : (k + 1) * group],
            residual_ref[...],
            (((0,), (0,)), ((), ())),
            preferred_element_type=jnp.float32,
        ).astype(jnp.bfloat16)


def gradient_blocks(scaled, mine, theirs, targets):
    block = (scaled.shape[1] // AXES["x"], mine.shape[1])
    return pl.pallas_call(
        gradient_kernel,
        out_shape=(in_vmem(block, jnp.bfloat16),) * AXES["x"],
        in_specs=[WHOLE] * 5,
        out_specs=(WHOLE,) * AXES["x"],
        scratch_shapes=[pltpu.VMEM(mine.shape, jnp.bfloat16)],
        compiler_params=pltpu.CompilerParams(vmem_limit_bytes=3 * VMEM_LIMIT),
        name="gradient",
    )(scaled, mine, theirs, *targets)


def collect_kernel(arrived_ref, gradient_ref, squares_ref):
    gradient = total([arrived_ref[k] for k in range(arrived_ref.shape[0])])
    gradient_ref[...] = gradient
    squares = jnp.sum(gradient * gradient, axis=0, keepdims=True)
    squares_ref[...] = jnp.broadcast_to(
        jnp.sum(squares, axis=1, keepdims=True), squares_ref.shape
    )


def collect(arrived):
    return pl.pallas_call(
        collect_kernel,
        out_shape=(
            jax.ShapeDtypeStruct(arrived.shape[1:], jnp.float32),
            jax.ShapeDtypeStruct((CHIPS * AXES["core"], LANES), jnp.float32),
        ),
        in_specs=[WHOLE],
        out_specs=(WHOLE, WHOLE),
        compiler_params=pltpu.CompilerParams(vmem_limit_bytes=VMEM_LIMIT),
        name="collect",
    )(arrived)


def clip_kernel(entries, squares_ref, gradient_ref, clipped_ref):
    mean_square = jnp.sum(squares_ref[...], axis=0, keepdims=True) / entries
    factor = jnp.minimum(1.0, lax.rsqrt(mean_square + epsilon))
    for j in range(gradient_ref.shape[1] // LANES):
        columns = slice(j * LANES, (j + 1) * LANES)
        clipped_ref[:, columns] = (gradient_ref[:, columns] * factor).astype(jnp.bfloat16)


def clip(squares, gradient, entries):
    return pl.pallas_call(
        functools.partial(clip_kernel, entries),
        out_shape=jax.ShapeDtypeStruct(gradient.shape, jnp.bfloat16),
        in_specs=[WHOLE, WHOLE],
        out_specs=WHOLE,
        compiler_params=pltpu.CompilerParams(vmem_limit_bytes=VMEM_LIMIT),
        name="clip",
    )(squares, gradient)


def shards(inputs, feature_gain, key_weight, teacher_keys, global_frag, local_frag, momentum):
    features = inputs.shape[2]
    rows, width = key_weight.shape[1:]

    column = spread(key_weight[0], "y_hi").reshape(AXES["y_hi"] * rows, width)
    raw = send(inputs[0], "core", 1)
    their_targets = send(teacher_keys[0], "core", 1)
    targets = (teacher_keys[0], their_targets)
    scaled = arrange(inputs[0], raw, feature_gain)
    column, scaled, targets, global_frag, local_frag = tied(
        column, scaled, targets, global_frag, local_frag
    )
    far = [column] + [send(column, "x", -k) for k in (1, 2, 3)]
    arrived = exchange(fragment_codes(global_frag, local_frag[0]), REPLICA)
    far, arrived = tied(far, arrived)
    partial = product(scaled, far)
    gradient = list(gradient_blocks(scaled, partial, send(partial, "core", 1), targets))
    gradient[0], arrived = tied(gradient[0], arrived)
    new_global, new_momentum = fragment_update(arrived, global_frag, momentum)
    mine = total([gradient[0]] + [send(gradient[k], "x", k) for k in STEPS])
    mine, new_global = tied(mine.astype(jnp.bfloat16), new_global)
    gradient, squares = collect(exchange(mine.reshape(AXES["y_hi"], rows, width), "y_hi"))

    clipped_grad = clip(exchange(squares, FSDP), gradient, features * width)[None]
    return (clipped_grad, new_global, new_momentum)


def solution(mesh):
    parted = Mesh(mesh.devices.reshape(tuple(AXES.values())), tuple(AXES))
    return jax.shard_map(
        shards,
        mesh=parted,
        in_specs=(
            P(REPLICA, FSDP, None),
            P(),
            P(REPLICA, FSDP, None),
            P(REPLICA, FSDP, None),
            P(FSDP),
            P(REPLICA, FSDP),
            P(FSDP + REPLICA),
        ),
        out_specs=(P(REPLICA, FSDP, None), P(FSDP), P(FSDP + REPLICA)),
        check_vma=False,
    )
```

```python
import functools

import jax
import jax.numpy as jnp
from jax import lax
from jax.experimental import pallas as pl
from jax.experimental.pallas import tpu as pltpu
from jax.sharding import Mesh
from jax.sharding import PartitionSpec as P

QBLOCK = 128
LANES = 128
VMEM_LIMIT = 8 << 20
WHOLE = pl.BlockSpec(memory_space=pltpu.VMEM)


outer_decay = 0.9
outer_rate = 0.7
clip_ratio = 2.0
epsilon = 1e-06

AXES = {"z": 8, "y_lo": 2, "y_hi": 4, "x": 4, "core": 2}
REPLICA = ("z", "y_lo")
FSDP = ("y_hi", "x", "core")
CHIPS = AXES["x"] * AXES["y_hi"]
STEPS = (2, 1, 3)


def send(value, axis, step):
    size = AXES[axis]
    return lax.ppermute(value, axis, [(i, (i + step) % size) for i in range(size)])


def tied(*values):
    return lax.optimization_barrier(values)


def arrange_kernel(order_ref, inputs_ref, theirs_ref, gain_ref, scaled_ref):
    for j in range(CHIPS):
        start = pl.multiple_of(order_ref[j] * LANES, LANES)
        columns = pl.ds(start, LANES)
        gain = gain_ref[:, columns]
        for half, ref in enumerate((inputs_ref, theirs_ref)):
            scaled_ref[half, :, j * LANES : (j + 1) * LANES] = (
                ref[:, columns].astype(jnp.float32) * gain
            ).astype(jnp.bfloat16)


def feature_order():
    x, core = lax.axis_index("x"), lax.axis_index("core")
    rx, y = jnp.arange(CHIPS) // AXES["y_hi"], jnp.arange(CHIPS) % AXES["y_hi"]
    chip = y * AXES["x"] + (x + rx) % AXES["x"]
    return (chip * 2 + core).astype(jnp.int32)


def arrange(order, inputs, theirs, feature_gain):
    tokens, features = inputs.shape
    step = 32
    block = pl.BlockSpec((step, features), lambda i: (i, 0))
    scaled = pl.pallas_call(
        arrange_kernel,
        grid=(tokens // step,),
        out_shape=jax.ShapeDtypeStruct((2, tokens, features // 2), jnp.bfloat16),
        in_specs=[
            pl.BlockSpec(memory_space=pltpu.SMEM),
            block,
            block,
            pl.BlockSpec((1, features), lambda i: (0, 0)),
        ],
        out_specs=pl.BlockSpec((2, step, features // 2), lambda i: (0, i, 0)),
        compiler_params=pltpu.CompilerParams(vmem_limit_bytes=6 * VMEM_LIMIT),
        name="arrange",
    )(order, inputs, theirs, feature_gain[None, :])
    return scaled.reshape(2 * tokens, features // 2)


def exchange(parts, axis):
    return lax.all_to_all(parts, axis, split_axis=0, concat_axis=0, tiled=True)


def copies_of(value, axis):
    return jnp.broadcast_to(value[None], (lax.axis_size(axis), *value.shape))


def total(values):
    return functools.reduce(jnp.add, [value.astype(jnp.float32) for value in values])


def codes_kernel(global_ref, local_ref, decoded_ref):
    difference = global_ref[...].astype(jnp.float32) - local_ref[...].astype(jnp.float32)
    mean = jnp.mean(difference * difference, axis=-1, keepdims=True)
    scales = (clip_ratio * jnp.sqrt(mean + epsilon)).astype(jnp.bfloat16).astype(jnp.float32)
    codes = jnp.clip(difference / scales, -1.0, 1.0).astype(jnp.bfloat16)
    decoded_ref[...] = (codes.astype(jnp.float32) * scales).astype(jnp.bfloat16)


def fragment_codes(global_frag, local_frag):
    step = min(256, global_frag.shape[0])
    block = pl.BlockSpec((step, QBLOCK), lambda i: (i, 0))
    return pl.pallas_call(
        codes_kernel,
        grid=(global_frag.shape[0] // step,),
        out_shape=jax.ShapeDtypeStruct(global_frag.shape, jnp.bfloat16),
        in_specs=[block, block],
        out_specs=block,
        compiler_params=pltpu.CompilerParams(vmem_limit_bytes=VMEM_LIMIT),
        name="codes",
    )(global_frag, local_frag)


def update_kernel(replica_ref, arrived_ref, momentum_ref, global_ref, momentum_out, copies_ref):
    replicas = arrived_ref.shape[0]
    pseudo = total([arrived_ref[i] for i in range(replicas)]) / replicas
    new_momentum = outer_decay * momentum_ref[...] + pseudo
    momentum_out[...] = new_momentum
    own_next = (
        global_ref[...].astype(jnp.float32)
        - outer_rate * (pseudo + outer_decay * new_momentum)
    ).astype(jnp.bfloat16)
    for i in range(replicas):
        copies_ref[i] = own_next


def fragment_update(replica, arrived, global_frag, momentum):
    replicas, rows = arrived.shape[:2]
    shares = pl.BlockSpec((replicas, rows, QBLOCK), lambda i, replica: (0, 0, 0))
    share = pl.BlockSpec((rows, QBLOCK), lambda i, replica: (0, 0))
    return pl.pallas_call(
        update_kernel,
        grid_spec=pltpu.PrefetchScalarGridSpec(
            num_scalar_prefetch=1,
            grid=(1,),
            in_specs=[
                shares,
                share,
                pl.BlockSpec((rows, QBLOCK), lambda i, replica: (replica[0], 0)),
            ],
            out_specs=(share, shares),
        ),
        out_shape=(
            jax.ShapeDtypeStruct((rows, QBLOCK), jnp.float32),
            jax.ShapeDtypeStruct(arrived.shape, jnp.bfloat16),
        ),
        compiler_params=pltpu.CompilerParams(vmem_limit_bytes=VMEM_LIMIT),
        name="update",
    )(replica, arrived, momentum, global_frag)


def in_vmem(shape, dtype):
    return pltpu.VMEM(shape, dtype)


def product_kernel(scaled_ref, *refs):
    *weight_refs, partial_ref = refs
    group = weight_refs[0].shape[0]
    partial_ref[...] = total(
        [
            jnp.dot(
                scaled_ref[:, k * group : (k + 1) * group],
                ref[...],
                preferred_element_type=jnp.float32,
            )
            for k, ref in enumerate(weight_refs)
        ]
    )


def product(scaled, weights):
    return pl.pallas_call(
        product_kernel,
        out_shape=in_vmem((scaled.shape[0], weights[0].shape[1]), jnp.float32),
        in_specs=[WHOLE] * (1 + len(weights)),
        out_specs=WHOLE,
        compiler_params=pltpu.CompilerParams(vmem_limit_bytes=2 * VMEM_LIMIT),
        name="product",
    )(scaled, *weights)


def gradient_kernel(scaled_ref, mine_ref, theirs_ref, *refs):
    *target_refs, first, second, third, fourth, residual_ref = refs
    tokens = target_refs[0].shape[0]
    for half, target_ref in enumerate(target_refs):
        here = slice(half * tokens, (half + 1) * tokens)
        there = slice((1 - half) * tokens, (2 - half) * tokens)
        residual_ref[here, :] = (
            mine_ref[here, :] + theirs_ref[there, :] - target_ref[...].astype(jnp.float32)
        ).astype(jnp.bfloat16)
    group = first.shape[0]
    for k, ref in enumerate((first, second, third, fourth)):
        ref[...] = lax.dot_general(
            scaled_ref[:, k * group : (k + 1) * group],
            residual_ref[...],
            (((0,), (0,)), ((), ())),
            preferred_element_type=jnp.float32,
        ).astype(jnp.bfloat16)


def gradient_blocks(scaled, mine, theirs, targets):
    block = (scaled.shape[1] // AXES["x"], mine.shape[1])
    return pl.pallas_call(
        gradient_kernel,
        out_shape=(in_vmem(block, jnp.bfloat16),) * AXES["x"],
        in_specs=[WHOLE] * 5,
        out_specs=(WHOLE,) * AXES["x"],
        scratch_shapes=[pltpu.VMEM(mine.shape, jnp.bfloat16)],
        compiler_params=pltpu.CompilerParams(vmem_limit_bytes=3 * VMEM_LIMIT),
        name="gradient",
    )(scaled, mine, theirs, *targets)


def collect_kernel(arrived_ref, gradient_ref, squares_ref):
    gradient = total([arrived_ref[k] for k in range(arrived_ref.shape[0])])
    gradient_ref[...] = gradient
    squares = jnp.sum(gradient * gradient, axis=0, keepdims=True)
    squares_ref[...] = jnp.broadcast_to(
        jnp.sum(squares, axis=1, keepdims=True), squares_ref.shape
    )


def collect(arrived):
    return pl.pallas_call(
        collect_kernel,
        out_shape=(
            jax.ShapeDtypeStruct(arrived.shape[1:], jnp.float32),
            jax.ShapeDtypeStruct((CHIPS * AXES["core"], LANES), jnp.float32),
        ),
        in_specs=[WHOLE],
        out_specs=(WHOLE, WHOLE),
        compiler_params=pltpu.CompilerParams(vmem_limit_bytes=VMEM_LIMIT),
        name="collect",
    )(arrived)


def clip_kernel(entries, squares_ref, gradient_ref, clipped_ref):
    mean_square = jnp.sum(squares_ref[...], axis=0, keepdims=True) / entries
    factor = jnp.minimum(1.0, lax.rsqrt(mean_square + epsilon))
    for j in range(gradient_ref.shape[1] // LANES):
        columns = slice(j * LANES, (j + 1) * LANES)
        clipped_ref[:, columns] = (gradient_ref[:, columns] * factor).astype(jnp.bfloat16)


def clip(squares, gradient, entries):
    return pl.pallas_call(
        functools.partial(clip_kernel, entries),
        out_shape=jax.ShapeDtypeStruct(gradient.shape, jnp.bfloat16),
        in_specs=[WHOLE, WHOLE],
        out_specs=WHOLE,
        compiler_params=pltpu.CompilerParams(vmem_limit_bytes=VMEM_LIMIT),
        name="clip",
    )(squares, gradient)


def shards(inputs, feature_gain, key_weight, teacher_keys, global_frag, local_frag, momentum):
    features = inputs.shape[2]
    rows, width = key_weight.shape[1:]
    replicas = lax.axis_size(REPLICA)
    replica = lax.axis_index(REPLICA).astype(jnp.int32)[None]
    global_frag = global_frag.reshape(-1, QBLOCK)
    local_frag = local_frag[0].reshape(-1, QBLOCK)
    momentum = momentum.reshape(-1, QBLOCK)
    key_weight, order, replica = tied(key_weight, feature_order(), replica)

    own, inputs, teacher_keys = tied(copies_of(key_weight[0], "y_hi"), inputs, teacher_keys)
    column = exchange(own, "y_hi").reshape(AXES["y_hi"] * rows, width)
    raw = send(inputs[0], "core", 1)
    targets = (teacher_keys[0], send(teacher_keys[0], "core", 1))
    scaled = arrange(order, inputs[0], raw, feature_gain)
    column, scaled, targets, global_frag, local_frag, replica = tied(
        column, scaled, targets, global_frag, local_frag, replica
    )
    far = [column] + [send(column, "x", -k) for k in (1, 2, 3)]
    decoded = fragment_codes(global_frag, local_frag)
    arrived = exchange(decoded.reshape(replicas, -1, QBLOCK), REPLICA)
    far, arrived = tied(far, arrived)
    partial = product(scaled, far)
    gradient = list(gradient_blocks(scaled, partial, send(partial, "core", 1), targets))
    gradient[0], arrived = tied(gradient[0], arrived)
    new_momentum, copies = fragment_update(replica, arrived, global_frag, momentum)
    new_global = exchange(copies, REPLICA)
    mine = total([gradient[0]] + [send(gradient[k], "x", k) for k in STEPS])
    mine, new_global = tied(mine.astype(jnp.bfloat16), new_global)
    gradient, squares = collect(exchange(mine.reshape(AXES["y_hi"], rows, width), "y_hi"))

    clipped_grad = clip(exchange(squares, FSDP), gradient, features * width)[None]
    return (clipped_grad, new_global.reshape(-1), new_momentum.reshape(-1))


def solution(mesh):
    parted = Mesh(mesh.devices.reshape(tuple(AXES.values())), tuple(AXES))
    return jax.shard_map(
        shards,
        mesh=parted,
        in_specs=(
            P(REPLICA, FSDP, None),
            P(),
            P(REPLICA, FSDP, None),
            P(REPLICA, FSDP, None),
            P(FSDP),
            P(REPLICA, FSDP),
            P(FSDP + REPLICA),
        ),
        out_specs=(P(REPLICA, FSDP, None), P(FSDP), P(FSDP + REPLICA)),
        check_vma=False,
    )
```

```python
import functools

import jax
import jax.numpy as jnp
from jax import lax
from jax.experimental import pallas as pl
from jax.experimental.pallas import tpu as pltpu
from jax.sharding import Mesh
from jax.sharding import PartitionSpec as P

QBLOCK = 128
LANES = 128
VMEM_LIMIT = 8 << 20
WHOLE = pl.BlockSpec(memory_space=pltpu.VMEM)


outer_decay = 0.9
outer_rate = 0.7
clip_ratio = 2.0
epsilon = 1e-06

AXES = {"z": 8, "y_lo": 2, "y_hi": 4, "x": 4, "core": 2}
REPLICA = ("z", "y_lo")
FSDP = ("y_hi", "x", "core")
CHIPS = AXES["x"] * AXES["y_hi"]
STEPS = (2, 1, 3)


def swap(value):
    return lax.ppermute(value, "core", [(0, 1), (1, 0)])


def send(value, wide, step):
    pairs = []
    for y in range(AXES["y_hi"]):
        for x in range(AXES["x"]):
            for core in range(AXES["core"]):
                to_y, to_x = y, x
                if (core == 0) == wide:
                    to_x = (x + step) % AXES["x"]
                else:
                    to_y = (y + step) % AXES["y_hi"]
                pairs.append(((y * AXES["x"] + x) * 2 + core, (to_y * AXES["x"] + to_x) * 2 + core))
    return lax.ppermute(value, FSDP, pairs)


def tied(*values):
    return lax.optimization_barrier(values)


def arrange_kernel(order_ref, inputs_ref, theirs_ref, gain_ref, scaled_ref):
    for j in range(CHIPS):
        start = pl.multiple_of(order_ref[j] * LANES, LANES)
        columns = pl.ds(start, LANES)
        gain = gain_ref[:, columns]
        for half, ref in enumerate((inputs_ref, theirs_ref)):
            scaled_ref[half, :, j * LANES : (j + 1) * LANES] = (
                ref[:, columns].astype(jnp.float32) * gain
            ).astype(jnp.bfloat16)


def feature_order():
    y, x, core = (lax.axis_index(name) for name in FSDP)
    wide, narrow = jnp.arange(CHIPS) // 4, jnp.arange(CHIPS) % 4
    to_y = (y + jnp.where(core == 0, narrow, wide)) % AXES["y_hi"]
    to_x = (x + jnp.where(core == 0, wide, narrow)) % AXES["x"]
    return ((to_y * AXES["x"] + to_x) * 2 + core).astype(jnp.int32)


def arrange(order, inputs, theirs, feature_gain):
    tokens, features = inputs.shape
    step = 96
    block = pl.BlockSpec((step, features), lambda i: (i, 0))
    scaled = pl.pallas_call(
        arrange_kernel,
        grid=(tokens // step,),
        out_shape=jax.ShapeDtypeStruct((2, tokens, features // 2), jnp.bfloat16),
        in_specs=[
            pl.BlockSpec(memory_space=pltpu.SMEM),
            block,
            block,
            pl.BlockSpec((1, features), lambda i: (0, 0)),
        ],
        out_specs=pl.BlockSpec((2, step, features // 2), lambda i: (0, i, 0)),
        compiler_params=pltpu.CompilerParams(vmem_limit_bytes=3 * VMEM_LIMIT),
        name="arrange",
    )(order, inputs, theirs, feature_gain[None, :])
    return scaled.reshape(2 * tokens, features // 2)


def exchange(parts, axis):
    return lax.all_to_all(parts, axis, split_axis=0, concat_axis=0, tiled=True)


def total(values):
    return functools.reduce(jnp.add, [value.astype(jnp.float32) for value in values])


def codes_kernel(global_ref, local_ref, decoded_ref):
    difference = global_ref[...].astype(jnp.float32) - local_ref[...].astype(jnp.float32)
    mean = jnp.mean(difference * difference, axis=-1, keepdims=True)
    scales = (clip_ratio * jnp.sqrt(mean + epsilon)).astype(jnp.bfloat16).astype(jnp.float32)
    codes = jnp.clip(difference / scales, -1.0, 1.0).astype(jnp.bfloat16)
    decoded_ref[...] = (codes.astype(jnp.float32) * scales).astype(jnp.bfloat16)


def fragment_codes(global_frag, local_frag):
    step = min(256, global_frag.shape[0])
    block = pl.BlockSpec((step, QBLOCK), lambda i: (i, 0))
    return pl.pallas_call(
        codes_kernel,
        grid=(global_frag.shape[0] // step,),
        out_shape=jax.ShapeDtypeStruct(global_frag.shape, jnp.bfloat16),
        in_specs=[block, block],
        out_specs=block,
        compiler_params=pltpu.CompilerParams(vmem_limit_bytes=VMEM_LIMIT),
        name="codes",
    )(global_frag, local_frag)


def update_kernel(replica_ref, arrived_ref, momentum_ref, global_ref, momentum_out, copies_ref):
    replicas = arrived_ref.shape[0]
    pseudo = total([arrived_ref[i] for i in range(replicas)]) / replicas
    new_momentum = outer_decay * momentum_ref[...] + pseudo
    momentum_out[...] = new_momentum
    own_next = (
        global_ref[...].astype(jnp.float32)
        - outer_rate * (pseudo + outer_decay * new_momentum)
    ).astype(jnp.bfloat16)
    for i in range(replicas):
        copies_ref[i] = own_next


def fragment_update(replica, arrived, global_frag, momentum):
    replicas, rows = arrived.shape[:2]
    shares = pl.BlockSpec((replicas, rows, QBLOCK), lambda i, replica: (0, 0, 0))
    share = pl.BlockSpec((rows, QBLOCK), lambda i, replica: (0, 0))
    return pl.pallas_call(
        update_kernel,
        grid_spec=pltpu.PrefetchScalarGridSpec(
            num_scalar_prefetch=1,
            grid=(1,),
            in_specs=[
                shares,
                share,
                pl.BlockSpec((rows, QBLOCK), lambda i, replica: (replica[0], 0)),
            ],
            out_specs=(share, shares),
        ),
        out_shape=(
            jax.ShapeDtypeStruct((rows, QBLOCK), jnp.float32),
            jax.ShapeDtypeStruct(arrived.shape, jnp.bfloat16),
        ),
        compiler_params=pltpu.CompilerParams(vmem_limit_bytes=VMEM_LIMIT),
        name="update",
    )(replica, arrived, momentum, global_frag)


def in_vmem(shape, dtype):
    return pltpu.VMEM(shape, dtype)


def product_kernel(scaled_ref, *refs):
    *weight_refs, partial_ref = refs
    group = weight_refs[0].shape[0]
    partial_ref[...] = total(
        [
            jnp.dot(
                scaled_ref[:, k * group : (k + 1) * group],
                ref[...],
                preferred_element_type=jnp.float32,
            )
            for k, ref in enumerate(weight_refs)
        ]
    )


def product(scaled, weights):
    return pl.pallas_call(
        product_kernel,
        out_shape=in_vmem((scaled.shape[0], weights[0].shape[1]), jnp.float32),
        in_specs=[WHOLE] * (1 + len(weights)),
        out_specs=WHOLE,
        compiler_params=pltpu.CompilerParams(vmem_limit_bytes=2 * VMEM_LIMIT),
        name="product",
    )(scaled, *weights)


def gradient_kernel(scaled_ref, mine_ref, theirs_ref, *refs):
    *target_refs, first, second, third, fourth, residual_ref = refs
    tokens = target_refs[0].shape[0]
    for half, target_ref in enumerate(target_refs):
        here = slice(half * tokens, (half + 1) * tokens)
        there = slice((1 - half) * tokens, (2 - half) * tokens)
        residual_ref[here, :] = (
            mine_ref[here, :] + theirs_ref[there, :] - target_ref[...].astype(jnp.float32)
        ).astype(jnp.bfloat16)
    group = first.shape[0]
    for k, ref in enumerate((first, second, third, fourth)):
        ref[...] = lax.dot_general(
            scaled_ref[:, k * group : (k + 1) * group],
            residual_ref[...],
            (((0,), (0,)), ((), ())),
            preferred_element_type=jnp.float32,
        ).astype(jnp.bfloat16)


def gradient_blocks(scaled, mine, theirs, targets):
    block = (scaled.shape[1] // AXES["x"], mine.shape[1])
    return pl.pallas_call(
        gradient_kernel,
        out_shape=(in_vmem(block, jnp.bfloat16),) * AXES["x"],
        in_specs=[WHOLE] * 5,
        out_specs=(WHOLE,) * AXES["x"],
        scratch_shapes=[pltpu.VMEM(mine.shape, jnp.bfloat16)],
        compiler_params=pltpu.CompilerParams(vmem_limit_bytes=3 * VMEM_LIMIT),
        name="gradient",
    )(scaled, mine, theirs, *targets)


def join_kernel(*refs):
    *part_refs, joined_ref = refs
    rows = part_refs[0].shape[0]
    for k, ref in enumerate(part_refs):
        joined_ref[k * rows : (k + 1) * rows, :] = ref[...]


def join(parts):
    rows, width = parts[0].shape
    return pl.pallas_call(
        join_kernel,
        out_shape=in_vmem((len(parts) * rows, width), parts[0].dtype),
        in_specs=[WHOLE] * len(parts),
        out_specs=WHOLE,
        compiler_params=pltpu.CompilerParams(vmem_limit_bytes=VMEM_LIMIT),
        name="join",
    )(*parts)


def add_kernel(first, second, third, fourth, *out_refs):
    rows = out_refs[0].shape[0]
    for k, ref in enumerate(out_refs):
        here = slice(k * rows, (k + 1) * rows)
        ref[...] = total([r[here, :] for r in (first, second, third, fourth)]).astype(jnp.bfloat16)


def add(blocks):
    rows, width = blocks[0].shape
    return pl.pallas_call(
        add_kernel,
        out_shape=(in_vmem((rows // 4, width), jnp.bfloat16),) * 4,
        in_specs=[WHOLE] * 4,
        out_specs=(WHOLE,) * 4,
        compiler_params=pltpu.CompilerParams(vmem_limit_bytes=VMEM_LIMIT),
        name="add",
    )(*blocks)


def collect_kernel(first, second, third, fourth, gradient_ref, squares_ref):
    gradient = total([ref[...] for ref in (first, second, third, fourth)])
    gradient_ref[...] = gradient
    squares = jnp.sum(gradient * gradient, axis=0, keepdims=True)
    squares_ref[...] = jnp.broadcast_to(
        jnp.sum(squares, axis=1, keepdims=True), squares_ref.shape
    )


def collect(blocks):
    return pl.pallas_call(
        collect_kernel,
        out_shape=(
            jax.ShapeDtypeStruct(blocks[0].shape, jnp.float32),
            jax.ShapeDtypeStruct((CHIPS * AXES["core"], LANES), jnp.float32),
        ),
        in_specs=[WHOLE] * 4,
        out_specs=(WHOLE, WHOLE),
        compiler_params=pltpu.CompilerParams(vmem_limit_bytes=VMEM_LIMIT),
        name="collect",
    )(*blocks)


def clip_kernel(entries, squares_ref, gradient_ref, clipped_ref):
    mean_square = jnp.sum(squares_ref[...], axis=0, keepdims=True) / entries
    factor = jnp.minimum(1.0, lax.rsqrt(mean_square + epsilon))
    for j in range(gradient_ref.shape[1] // LANES):
        columns = slice(j * LANES, (j + 1) * LANES)
        clipped_ref[:, columns] = (gradient_ref[:, columns] * factor).astype(jnp.bfloat16)


def clip(squares, gradient, entries):
    return pl.pallas_call(
        functools.partial(clip_kernel, entries),
        out_shape=jax.ShapeDtypeStruct(gradient.shape, jnp.bfloat16),
        in_specs=[WHOLE, WHOLE],
        out_specs=WHOLE,
        compiler_params=pltpu.CompilerParams(vmem_limit_bytes=VMEM_LIMIT),
        name="clip",
    )(squares, gradient)


def shards(inputs, feature_gain, key_weight, teacher_keys, global_frag, local_frag, momentum):
    features = inputs.shape[2]
    rows, width = key_weight.shape[1:]
    replicas = lax.axis_size(REPLICA)
    replica = lax.axis_index(REPLICA).astype(jnp.int32)[None]
    global_frag = global_frag.reshape(-1, QBLOCK)
    local_frag = local_frag[0].reshape(-1, QBLOCK)
    momentum = momentum.reshape(-1, QBLOCK)
    key_weight, order, replica = tied(key_weight, feature_order(), replica)

    weight = key_weight[0]
    column = join([weight] + [send(weight, False, -k) for k in (1, 2, 3)])
    raw = swap(inputs[0])
    targets = (teacher_keys[0], swap(teacher_keys[0]))
    column, targets, global_frag, local_frag, replica = tied(
        column, targets, global_frag, local_frag, replica
    )
    far = [column] + [send(column, True, -k) for k in (1, 2, 3)]
    decoded = fragment_codes(global_frag, local_frag)
    scaled = arrange(order, inputs[0], raw, feature_gain)
    decoded, scaled = tied(decoded, scaled)
    arrived = exchange(decoded.reshape(replicas, -1, QBLOCK), REPLICA)
    far, arrived = tied(far, arrived)
    partial = product(scaled, far)
    gradient = list(gradient_blocks(scaled, partial, swap(partial), targets))
    gradient[0], arrived = tied(gradient[0], arrived)
    new_momentum, copies = fragment_update(replica, arrived, global_frag, momentum)
    new_global = exchange(copies, REPLICA)
    mine = add([gradient[0]] + [send(gradient[k], True, k) for k in STEPS])
    mine, new_global = tied(mine, new_global)
    gradient, squares = collect([mine[0]] + [send(mine[k], False, k) for k in STEPS])

    clipped_grad = clip(exchange(squares, FSDP), gradient, features * width)[None]
    return (clipped_grad, new_global.reshape(-1), new_momentum.reshape(-1))


def solution(mesh):
    parted = Mesh(mesh.devices.reshape(tuple(AXES.values())), tuple(AXES))
    return jax.shard_map(
        shards,
        mesh=parted,
        in_specs=(
            P(REPLICA, FSDP, None),
            P(),
            P(REPLICA, FSDP, None),
            P(REPLICA, FSDP, None),
            P(FSDP),
            P(REPLICA, FSDP),
            P(FSDP + REPLICA),
        ),
        out_specs=(P(REPLICA, FSDP, None), P(FSDP), P(FSDP + REPLICA)),
        check_vma=False,
    )
```

```python
import functools

import jax
import jax.numpy as jnp
from jax import lax
from jax.experimental import pallas as pl
from jax.experimental.pallas import tpu as pltpu
from jax.sharding import Mesh
from jax.sharding import PartitionSpec as P

QBLOCK = 128
LANES = 128
VMEM_LIMIT = 8 << 20
WHOLE = pl.BlockSpec(memory_space=pltpu.VMEM)


outer_decay = 0.9
outer_rate = 0.7
clip_ratio = 2.0
epsilon = 1e-06

AXES = {"z": 8, "y_lo": 2, "y_hi": 4, "x": 4, "core": 2}
REPLICA = ("z", "y_lo")
FSDP = ("y_hi", "x", "core")
CHIPS = AXES["x"] * AXES["y_hi"]
STEPS = (2, 1, 3)


def send(value, axis, step):
    size = AXES[axis]
    return lax.ppermute(value, axis, [(i, (i + step) % size) for i in range(size)])


def deliver(value, wide, step):
    pairs = []
    for y in range(AXES["y_hi"]):
        for x in range(AXES["x"]):
            for core in range(AXES["core"]):
                to_y, to_x = y, x
                if (core == 0) == wide:
                    to_x = (x + step) % AXES["x"]
                else:
                    to_y = (y + step) % AXES["y_hi"]
                pairs.append(((y * AXES["x"] + x) * 2 + core, (to_y * AXES["x"] + to_x) * 2 + core))
    return lax.ppermute(value, FSDP, pairs)


def tied(*values):
    return lax.optimization_barrier(values)


def arrange_kernel(order_ref, inputs_ref, theirs_ref, gain_ref, scaled_ref):
    for j in range(CHIPS):
        start = pl.multiple_of(order_ref[j] * LANES, LANES)
        columns = pl.ds(start, LANES)
        gain = gain_ref[:, columns]
        for half, ref in enumerate((inputs_ref, theirs_ref)):
            scaled_ref[half, :, j * LANES : (j + 1) * LANES] = (
                ref[:, columns].astype(jnp.float32) * gain
            ).astype(jnp.bfloat16)


def feature_order():
    x, core = lax.axis_index("x"), lax.axis_index("core")
    rx, y = jnp.arange(CHIPS) // AXES["y_hi"], jnp.arange(CHIPS) % AXES["y_hi"]
    chip = y * AXES["x"] + (x + rx) % AXES["x"]
    return (chip * 2 + core).astype(jnp.int32)


def block_order():
    y, core = lax.axis_index("y_hi"), lax.axis_index("core")
    wide, narrow = jnp.arange(CHIPS) // 4, jnp.arange(CHIPS) % 4
    to_y = (y + jnp.where(core == 0, narrow, wide)) % AXES["y_hi"]
    to_x = jnp.where(core == 0, wide, narrow)
    return (to_x * AXES["y_hi"] + to_y).astype(jnp.int32)


def arrange(order, inputs, theirs, feature_gain):
    tokens, features = inputs.shape
    step = 96
    block = pl.BlockSpec((step, features), lambda i: (i, 0))
    scaled = pl.pallas_call(
        arrange_kernel,
        grid=(tokens // step,),
        out_shape=jax.ShapeDtypeStruct((2, tokens, features // 2), jnp.bfloat16),
        in_specs=[
            pl.BlockSpec(memory_space=pltpu.SMEM),
            block,
            block,
            pl.BlockSpec((1, features), lambda i: (0, 0)),
        ],
        out_specs=pl.BlockSpec((2, step, features // 2), lambda i: (0, i, 0)),
        compiler_params=pltpu.CompilerParams(vmem_limit_bytes=6 * VMEM_LIMIT),
        name="arrange",
    )(order, inputs, theirs, feature_gain[None, :])
    return scaled.reshape(2 * tokens, features // 2)


def exchange(parts, axis):
    return lax.all_to_all(parts, axis, split_axis=0, concat_axis=0, tiled=True)


def copies_of(value, axis):
    return jnp.broadcast_to(value[None], (lax.axis_size(axis), *value.shape))


def total(values):
    return functools.reduce(jnp.add, [value.astype(jnp.float32) for value in values])


def codes_kernel(global_ref, local_ref, decoded_ref):
    difference = global_ref[...].astype(jnp.float32) - local_ref[...].astype(jnp.float32)
    mean = jnp.mean(difference * difference, axis=-1, keepdims=True)
    scales = (clip_ratio * jnp.sqrt(mean + epsilon)).astype(jnp.bfloat16).astype(jnp.float32)
    codes = jnp.clip(difference / scales, -1.0, 1.0).astype(jnp.bfloat16)
    decoded_ref[...] = (codes.astype(jnp.float32) * scales).astype(jnp.bfloat16)


def fragment_codes(global_frag, local_frag):
    step = min(256, global_frag.shape[0])
    block = pl.BlockSpec((step, QBLOCK), lambda i: (i, 0))
    return pl.pallas_call(
        codes_kernel,
        grid=(global_frag.shape[0] // step,),
        out_shape=jax.ShapeDtypeStruct(global_frag.shape, jnp.bfloat16),
        in_specs=[block, block],
        out_specs=block,
        compiler_params=pltpu.CompilerParams(vmem_limit_bytes=VMEM_LIMIT),
        name="codes",
    )(global_frag, local_frag)


def update_kernel(replica_ref, arrived_ref, momentum_ref, global_ref, momentum_out, copies_ref):
    replicas = arrived_ref.shape[0]
    pseudo = total([arrived_ref[i] for i in range(replicas)]) / replicas
    new_momentum = outer_decay * momentum_ref[...] + pseudo
    momentum_out[...] = new_momentum
    own_next = (
        global_ref[...].astype(jnp.float32)
        - outer_rate * (pseudo + outer_decay * new_momentum)
    ).astype(jnp.bfloat16)
    for i in range(replicas):
        copies_ref[i] = own_next


def fragment_update(replica, arrived, global_frag, momentum):
    replicas, rows = arrived.shape[:2]
    shares = pl.BlockSpec((replicas, rows, QBLOCK), lambda i, replica: (0, 0, 0))
    share = pl.BlockSpec((rows, QBLOCK), lambda i, replica: (0, 0))
    return pl.pallas_call(
        update_kernel,
        grid_spec=pltpu.PrefetchScalarGridSpec(
            num_scalar_prefetch=1,
            grid=(1,),
            in_specs=[
                shares,
                share,
                pl.BlockSpec((rows, QBLOCK), lambda i, replica: (replica[0], 0)),
            ],
            out_specs=(share, shares),
        ),
        out_shape=(
            jax.ShapeDtypeStruct((rows, QBLOCK), jnp.float32),
            jax.ShapeDtypeStruct(arrived.shape, jnp.bfloat16),
        ),
        compiler_params=pltpu.CompilerParams(vmem_limit_bytes=VMEM_LIMIT),
        name="update",
    )(replica, arrived, momentum, global_frag)


def in_vmem(shape, dtype):
    return pltpu.VMEM(shape, dtype)


def product_kernel(scaled_ref, *refs):
    *weight_refs, partial_ref = refs
    group = weight_refs[0].shape[0]
    partial_ref[...] = total(
        [
            jnp.dot(
                scaled_ref[:, k * group : (k + 1) * group],
                ref[...],
                preferred_element_type=jnp.float32,
            )
            for k, ref in enumerate(weight_refs)
        ]
    )


def product(scaled, weights):
    return pl.pallas_call(
        product_kernel,
        out_shape=in_vmem((scaled.shape[0], weights[0].shape[1]), jnp.float32),
        in_specs=[WHOLE] * (1 + len(weights)),
        out_specs=WHOLE,
        compiler_params=pltpu.CompilerParams(vmem_limit_bytes=2 * VMEM_LIMIT),
        name="product",
    )(scaled, *weights)


def gradient_kernel(order_ref, scaled_ref, mine_ref, theirs_ref, *refs):
    *target_refs, first, second, third, fourth, residual_ref, columns_ref = refs
    tokens = target_refs[0].shape[0]
    for half, target_ref in enumerate(target_refs):
        here = slice(half * tokens, (half + 1) * tokens)
        there = slice((1 - half) * tokens, (2 - half) * tokens)
        residual_ref[here, :] = (
            mine_ref[here, :] + theirs_ref[there, :] - target_ref[...].astype(jnp.float32)
        ).astype(jnp.bfloat16)
    parts = first.shape[0] // LANES
    for k, ref in enumerate((first, second, third, fourth)):
        for j in range(parts):
            start = pl.multiple_of(order_ref[k * parts + j] * LANES, LANES)
            columns_ref[:, j * LANES : (j + 1) * LANES] = scaled_ref[:, pl.ds(start, LANES)]
        ref[...] = lax.dot_general(
            columns_ref[...],
            residual_ref[...],
            (((0,), (0,)), ((), ())),
            preferred_element_type=jnp.float32,
        ).astype(jnp.bfloat16)


def gradient_blocks(order, scaled, mine, theirs, targets):
    block = (scaled.shape[1] // AXES["x"], mine.shape[1])
    return pl.pallas_call(
        gradient_kernel,
        out_shape=(in_vmem(block, jnp.bfloat16),) * AXES["x"],
        in_specs=[pl.BlockSpec(memory_space=pltpu.SMEM)] + [WHOLE] * 5,
        out_specs=(WHOLE,) * AXES["x"],
        scratch_shapes=[
            pltpu.VMEM(mine.shape, jnp.bfloat16),
            pltpu.VMEM((scaled.shape[0], block[0]), jnp.bfloat16),
        ],
        compiler_params=pltpu.CompilerParams(vmem_limit_bytes=3 * VMEM_LIMIT),
        name="gradient",
    )(order, scaled, mine, theirs, *targets)


def add_kernel(first, second, third, fourth, *out_refs):
    rows = out_refs[0].shape[0]
    for k, ref in enumerate(out_refs):
        here = slice(k * rows, (k + 1) * rows)
        ref[...] = total([r[here, :] for r in (first, second, third, fourth)]).astype(jnp.bfloat16)


def add(blocks):
    rows, width = blocks[0].shape
    return pl.pallas_call(
        add_kernel,
        out_shape=(in_vmem((rows // 4, width), jnp.bfloat16),) * 4,
        in_specs=[WHOLE] * 4,
        out_specs=(WHOLE,) * 4,
        compiler_params=pltpu.CompilerParams(vmem_limit_bytes=VMEM_LIMIT),
        name="add",
    )(*blocks)


def collect_kernel(first, second, third, fourth, gradient_ref, squares_ref):
    gradient = total([ref[...] for ref in (first, second, third, fourth)])
    gradient_ref[...] = gradient
    squares = jnp.sum(gradient * gradient, axis=0, keepdims=True)
    squares_ref[...] = jnp.broadcast_to(
        jnp.sum(squares, axis=1, keepdims=True), squares_ref.shape
    )


def collect(blocks):
    return pl.pallas_call(
        collect_kernel,
        out_shape=(
            jax.ShapeDtypeStruct(blocks[0].shape, jnp.float32),
            jax.ShapeDtypeStruct((CHIPS * AXES["core"], LANES), jnp.float32),
        ),
        in_specs=[WHOLE] * 4,
        out_specs=(WHOLE, WHOLE),
        compiler_params=pltpu.CompilerParams(vmem_limit_bytes=VMEM_LIMIT),
        name="collect",
    )(*blocks)


def clip_kernel(entries, squares_ref, gradient_ref, clipped_ref):
    mean_square = jnp.sum(squares_ref[...], axis=0, keepdims=True) / entries
    factor = jnp.minimum(1.0, lax.rsqrt(mean_square + epsilon))
    for j in range(gradient_ref.shape[1] // LANES):
        columns = slice(j * LANES, (j + 1) * LANES)
        clipped_ref[:, columns] = (gradient_ref[:, columns] * factor).astype(jnp.bfloat16)


def clip(squares, gradient, entries):
    return pl.pallas_call(
        functools.partial(clip_kernel, entries),
        out_shape=jax.ShapeDtypeStruct(gradient.shape, jnp.bfloat16),
        in_specs=[WHOLE, WHOLE],
        out_specs=WHOLE,
        compiler_params=pltpu.CompilerParams(vmem_limit_bytes=VMEM_LIMIT),
        name="clip",
    )(squares, gradient)


def shards(inputs, feature_gain, key_weight, teacher_keys, global_frag, local_frag, momentum):
    features = inputs.shape[2]
    rows, width = key_weight.shape[1:]
    replicas = lax.axis_size(REPLICA)
    replica = lax.axis_index(REPLICA).astype(jnp.int32)[None]
    global_frag = global_frag.reshape(-1, QBLOCK)
    local_frag = local_frag[0].reshape(-1, QBLOCK)
    momentum = momentum.reshape(-1, QBLOCK)
    key_weight, order, blocks, replica = tied(
        key_weight, feature_order(), block_order(), replica
    )

    own, inputs, teacher_keys = tied(copies_of(key_weight[0], "y_hi"), inputs, teacher_keys)
    column = exchange(own, "y_hi").reshape(AXES["y_hi"] * rows, width)
    raw = send(inputs[0], "core", 1)
    targets = (teacher_keys[0], send(teacher_keys[0], "core", 1))
    scaled = arrange(order, inputs[0], raw, feature_gain)
    column, scaled, targets, global_frag, local_frag, replica, blocks = tied(
        column, scaled, targets, global_frag, local_frag, replica, blocks
    )
    far = [column] + [send(column, "x", -k) for k in (1, 2, 3)]
    decoded = fragment_codes(global_frag, local_frag)
    arrived = exchange(decoded.reshape(replicas, -1, QBLOCK), REPLICA)
    far, arrived = tied(far, arrived)
    partial = product(scaled, far)
    gradient = list(gradient_blocks(blocks, scaled, partial, send(partial, "core", 1), targets))
    gradient[0], arrived = tied(gradient[0], arrived)
    new_momentum, copies = fragment_update(replica, arrived, global_frag, momentum)
    new_global = exchange(copies, REPLICA)
    mine = add([gradient[0]] + [deliver(gradient[k], True, k) for k in STEPS])
    mine, new_global = tied(mine, new_global)
    gradient, squares = collect([mine[0]] + [deliver(mine[k], False, k) for k in STEPS])

    clipped_grad = clip(exchange(squares, FSDP), gradient, features * width)[None]
    return (clipped_grad, new_global.reshape(-1), new_momentum.reshape(-1))


def solution(mesh):
    parted = Mesh(mesh.devices.reshape(tuple(AXES.values())), tuple(AXES))
    return jax.shard_map(
        shards,
        mesh=parted,
        in_specs=(
            P(REPLICA, FSDP, None),
            P(),
            P(REPLICA, FSDP, None),
            P(REPLICA, FSDP, None),
            P(FSDP),
            P(REPLICA, FSDP),
            P(FSDP + REPLICA),
        ),
        out_specs=(P(REPLICA, FSDP, None), P(FSDP), P(FSDP + REPLICA)),
        check_vma=False,
    )
```

```python
import functools

import jax
import jax.numpy as jnp
from jax import lax
from jax.experimental import pallas as pl
from jax.experimental.pallas import tpu as pltpu
from jax.sharding import Mesh
from jax.sharding import PartitionSpec as P

QBLOCK = 128
LANES = 128
VMEM_LIMIT = 8 << 20
WHOLE = pl.BlockSpec(memory_space=pltpu.VMEM)


outer_decay = 0.9
outer_rate = 0.7
clip_ratio = 2.0
epsilon = 1e-06

AXES = {"z": 8, "y_lo": 2, "y_hi": 4, "x": 4, "core": 2}
REPLICA = ("z", "y_lo")
FSDP = ("y_hi", "x", "core")
CHIPS = AXES["x"] * AXES["y_hi"]
STEPS = (2, 1, 3)


def send(value, axis, step):
    size = AXES[axis]
    return lax.ppermute(value, axis, [(i, (i + step) % size) for i in range(size)])


def tied(*values):
    return lax.optimization_barrier(values)


def arrange_kernel(order_ref, inputs_ref, theirs_ref, gain_ref, scaled_ref):
    for j in range(CHIPS):
        start = pl.multiple_of(order_ref[j] * LANES, LANES)
        columns = pl.ds(start, LANES)
        gain = gain_ref[:, columns]
        for half, ref in enumerate((inputs_ref, theirs_ref)):
            scaled_ref[half, :, j * LANES : (j + 1) * LANES] = (
                ref[:, columns].astype(jnp.float32) * gain
            ).astype(jnp.bfloat16)


def feature_order():
    x, core = lax.axis_index("x"), lax.axis_index("core")
    rx, y = jnp.arange(CHIPS) // AXES["y_hi"], jnp.arange(CHIPS) % AXES["y_hi"]
    chip = y * AXES["x"] + (x + rx) % AXES["x"]
    return (chip * 2 + core).astype(jnp.int32)


def arrange(order, inputs, theirs, feature_gain):
    tokens, features = inputs.shape
    step = 96
    block = pl.BlockSpec((step, features), lambda i: (i, 0))
    scaled = pl.pallas_call(
        arrange_kernel,
        grid=(tokens // step,),
        out_shape=jax.ShapeDtypeStruct((2, tokens, features // 2), jnp.bfloat16),
        in_specs=[
            pl.BlockSpec(memory_space=pltpu.SMEM),
            block,
            block,
            pl.BlockSpec((1, features), lambda i: (0, 0)),
        ],
        out_specs=pl.BlockSpec((2, step, features // 2), lambda i: (0, i, 0)),
        compiler_params=pltpu.CompilerParams(vmem_limit_bytes=6 * VMEM_LIMIT),
        name="arrange",
    )(order, inputs, theirs, feature_gain[None, :])
    return scaled.reshape(2 * tokens, features // 2)


def exchange(parts, axis):
    return lax.all_to_all(parts, axis, split_axis=0, concat_axis=0, tiled=True)


def copies_of(value, axis):
    return jnp.broadcast_to(value[None], (lax.axis_size(axis), *value.shape))


def total(values):
    return functools.reduce(jnp.add, [value.astype(jnp.float32) for value in values])


def codes_kernel(global_ref, local_ref, decoded_ref):
    difference = global_ref[...].astype(jnp.float32) - local_ref[...].astype(jnp.float32)
    mean = jnp.mean(difference * difference, axis=-1, keepdims=True)
    scales = (clip_ratio * jnp.sqrt(mean + epsilon)).astype(jnp.bfloat16).astype(jnp.float32)
    codes = jnp.clip(difference / scales, -1.0, 1.0).astype(jnp.bfloat16)
    decoded_ref[...] = (codes.astype(jnp.float32) * scales).astype(jnp.bfloat16)


def fragment_codes(global_frag, local_frag):
    step = min(256, global_frag.shape[0])
    block = pl.BlockSpec((step, QBLOCK), lambda i: (i, 0))
    return pl.pallas_call(
        codes_kernel,
        grid=(global_frag.shape[0] // step,),
        out_shape=jax.ShapeDtypeStruct(global_frag.shape, jnp.bfloat16),
        in_specs=[block, block],
        out_specs=block,
        compiler_params=pltpu.CompilerParams(vmem_limit_bytes=VMEM_LIMIT),
        name="codes",
    )(global_frag, local_frag)


def update_kernel(replica_ref, arrived_ref, momentum_ref, global_ref, momentum_out, copies_ref):
    replicas = arrived_ref.shape[0]
    pseudo = total([arrived_ref[i] for i in range(replicas)]) / replicas
    new_momentum = outer_decay * momentum_ref[...] + pseudo
    momentum_out[...] = new_momentum
    own_next = (
        global_ref[...].astype(jnp.float32)
        - outer_rate * (pseudo + outer_decay * new_momentum)
    ).astype(jnp.bfloat16)
    for i in range(replicas):
        copies_ref[i] = own_next


def fragment_update(replica, arrived, global_frag, momentum):
    replicas, rows = arrived.shape[:2]
    shares = pl.BlockSpec((replicas, rows, QBLOCK), lambda i, replica: (0, 0, 0))
    share = pl.BlockSpec((rows, QBLOCK), lambda i, replica: (0, 0))
    return pl.pallas_call(
        update_kernel,
        grid_spec=pltpu.PrefetchScalarGridSpec(
            num_scalar_prefetch=1,
            grid=(1,),
            in_specs=[
                shares,
                share,
                pl.BlockSpec((rows, QBLOCK), lambda i, replica: (replica[0], 0)),
            ],
            out_specs=(share, shares),
        ),
        out_shape=(
            jax.ShapeDtypeStruct((rows, QBLOCK), jnp.float32),
            jax.ShapeDtypeStruct(arrived.shape, jnp.bfloat16),
        ),
        compiler_params=pltpu.CompilerParams(vmem_limit_bytes=VMEM_LIMIT),
        name="update",
    )(replica, arrived, momentum, global_frag)


def in_vmem(shape, dtype):
    return pltpu.VMEM(shape, dtype)


def product_kernel(scaled_ref, *refs):
    *weight_refs, partial_ref = refs
    group = weight_refs[0].shape[0]
    partial_ref[...] = total(
        [
            jnp.dot(
                scaled_ref[:, k * group : (k + 1) * group],
                ref[...],
                preferred_element_type=jnp.float32,
            )
            for k, ref in enumerate(weight_refs)
        ]
    )


def product(scaled, weights):
    return pl.pallas_call(
        product_kernel,
        out_shape=in_vmem((scaled.shape[0], weights[0].shape[1]), jnp.float32),
        in_specs=[WHOLE] * (1 + len(weights)),
        out_specs=WHOLE,
        compiler_params=pltpu.CompilerParams(vmem_limit_bytes=2 * VMEM_LIMIT),
        name="product",
    )(scaled, *weights)


def gradient_kernel(scaled_ref, mine_ref, theirs_ref, *refs):
    *target_refs, first, second, third, fourth, residual_ref = refs
    tokens = target_refs[0].shape[0]
    for half, target_ref in enumerate(target_refs):
        here = slice(half * tokens, (half + 1) * tokens)
        there = slice((1 - half) * tokens, (2 - half) * tokens)
        residual_ref[here, :] = (
            mine_ref[here, :] + theirs_ref[there, :] - target_ref[...].astype(jnp.float32)
        ).astype(jnp.bfloat16)
    group = first.shape[0]
    for k, ref in enumerate((first, second, third, fourth)):
        ref[...] = lax.dot_general(
            scaled_ref[:, k * group : (k + 1) * group],
            residual_ref[...],
            (((0,), (0,)), ((), ())),
            preferred_element_type=jnp.float32,
        ).astype(jnp.bfloat16)


def gradient_blocks(scaled, mine, theirs, targets):
    block = (scaled.shape[1] // AXES["x"], mine.shape[1])
    return pl.pallas_call(
        gradient_kernel,
        out_shape=(jax.ShapeDtypeStruct(block, jnp.bfloat16),) * AXES["x"],
        in_specs=[WHOLE] * 5,
        out_specs=(WHOLE,) * AXES["x"],
        scratch_shapes=[pltpu.VMEM(mine.shape, jnp.bfloat16)],
        compiler_params=pltpu.CompilerParams(vmem_limit_bytes=3 * VMEM_LIMIT),
        name="gradient",
    )(scaled, mine, theirs, *targets)


def add_kernel(first, second, third, fourth, sum_ref):
    sum_ref[...] = total([ref[...] for ref in (first, second, third, fourth)]).astype(
        jnp.bfloat16
    )


def add(blocks):
    return pl.pallas_call(
        add_kernel,
        out_shape=jax.ShapeDtypeStruct(blocks[0].shape, jnp.bfloat16),
        in_specs=[WHOLE] * 4,
        out_specs=WHOLE,
        compiler_params=pltpu.CompilerParams(vmem_limit_bytes=VMEM_LIMIT),
        name="add",
    )(*blocks)


def place_kernel(value_ref, placed_ref):
    placed_ref[...] = value_ref[...]


def place(value):
    step = value.shape[0] // 4
    block = pl.BlockSpec((step, value.shape[1]), lambda i: (i, 0))
    return pl.pallas_call(
        place_kernel,
        grid=(4,),
        out_shape=jax.ShapeDtypeStruct(value.shape, value.dtype),
        in_specs=[block],
        out_specs=block,
        compiler_params=pltpu.CompilerParams(vmem_limit_bytes=VMEM_LIMIT),
        name="place",
    )(value)


def collect_kernel(arrived_ref, gradient_ref, squares_ref):
    gradient = total([arrived_ref[k] for k in range(arrived_ref.shape[0])])
    gradient_ref[...] = gradient
    squares = jnp.sum(gradient * gradient, axis=0, keepdims=True)
    squares_ref[...] = jnp.broadcast_to(
        jnp.sum(squares, axis=1, keepdims=True), squares_ref.shape
    )


def collect(arrived):
    return pl.pallas_call(
        collect_kernel,
        out_shape=(
            jax.ShapeDtypeStruct(arrived.shape[1:], jnp.float32),
            jax.ShapeDtypeStruct((CHIPS * AXES["core"], LANES), jnp.float32),
        ),
        in_specs=[WHOLE],
        out_specs=(WHOLE, WHOLE),
        compiler_params=pltpu.CompilerParams(vmem_limit_bytes=VMEM_LIMIT),
        name="collect",
    )(arrived)


def clip_kernel(entries, squares_ref, gradient_ref, clipped_ref):
    mean_square = jnp.sum(squares_ref[...], axis=0, keepdims=True) / entries
    factor = jnp.minimum(1.0, lax.rsqrt(mean_square + epsilon))
    for j in range(gradient_ref.shape[1] // LANES):
        columns = slice(j * LANES, (j + 1) * LANES)
        clipped_ref[:, columns] = (gradient_ref[:, columns] * factor).astype(jnp.bfloat16)


def clip(squares, gradient, entries):
    return pl.pallas_call(
        functools.partial(clip_kernel, entries),
        out_shape=jax.ShapeDtypeStruct(gradient.shape, jnp.bfloat16),
        in_specs=[WHOLE, WHOLE],
        out_specs=WHOLE,
        compiler_params=pltpu.CompilerParams(vmem_limit_bytes=VMEM_LIMIT),
        name="clip",
    )(squares, gradient)


def shards(inputs, feature_gain, key_weight, teacher_keys, global_frag, local_frag, momentum):
    features = inputs.shape[2]
    rows, width = key_weight.shape[1:]
    replicas = lax.axis_size(REPLICA)
    replica = lax.axis_index(REPLICA).astype(jnp.int32)[None]
    global_frag = global_frag.reshape(-1, QBLOCK)
    local_frag = local_frag[0].reshape(-1, QBLOCK)
    momentum = momentum.reshape(-1, QBLOCK)
    key_weight, order, replica = tied(key_weight, feature_order(), replica)

    own, inputs, teacher_keys = tied(copies_of(key_weight[0], "y_hi"), inputs, teacher_keys)
    column = exchange(own, "y_hi").reshape(AXES["y_hi"] * rows, width)
    raw = send(inputs[0], "core", 1)
    targets = (teacher_keys[0], send(teacher_keys[0], "core", 1))
    scaled = arrange(order, inputs[0], raw, feature_gain)
    column, scaled, targets, global_frag, local_frag, replica = tied(
        column, scaled, targets, global_frag, local_frag, replica
    )
    far = [column] + [send(column, "x", -k) for k in (1, 2, 3)]
    decoded = fragment_codes(global_frag, local_frag)
    arrived = exchange(decoded.reshape(replicas, -1, QBLOCK), REPLICA)
    far, arrived = tied(far, arrived)
    partial = product(scaled, far)
    gradient = list(gradient_blocks(scaled, partial, send(partial, "core", 1), targets))
    gradient[0], arrived = tied(gradient[0], arrived)
    new_momentum, copies = fragment_update(replica, arrived, global_frag, momentum)
    new_global = exchange(copies, REPLICA)
    mine = add([gradient[0]] + [send(gradient[k], "x", k) for k in STEPS])
    mine, new_global = tied(mine, new_global)
    gradient, squares = collect(exchange(mine.reshape(AXES["y_hi"], rows, width), "y_hi"))

    squares, new_global = tied(squares, new_global)
    new_global = place(new_global.reshape(-1, QBLOCK))
    clipped_grad = clip(exchange(squares, FSDP), gradient, features * width)[None]
    return (clipped_grad, new_global.reshape(-1), new_momentum.reshape(-1))


def solution(mesh):
    parted = Mesh(mesh.devices.reshape(tuple(AXES.values())), tuple(AXES))
    return jax.shard_map(
        shards,
        mesh=parted,
        in_specs=(
            P(REPLICA, FSDP, None),
            P(),
            P(REPLICA, FSDP, None),
            P(REPLICA, FSDP, None),
            P(FSDP),
            P(REPLICA, FSDP),
            P(FSDP + REPLICA),
        ),
        out_specs=(P(REPLICA, FSDP, None), P(FSDP), P(FSDP + REPLICA)),
        check_vma=False,
    )
```

```python
import functools

import jax
import jax.numpy as jnp
from jax import lax
from jax.experimental import pallas as pl
from jax.experimental.pallas import tpu as pltpu
from jax.sharding import Mesh
from jax.sharding import PartitionSpec as P

QBLOCK = 128
LANES = 128
VMEM_LIMIT = 8 << 20
WHOLE = pl.BlockSpec(memory_space=pltpu.VMEM)


outer_decay = 0.9
outer_rate = 0.7
clip_ratio = 2.0
epsilon = 1e-06

AXES = {"z": 8, "y_lo": 2, "y_hi": 4, "x": 4, "core": 2}
REPLICA = ("z", "y_lo")
FSDP = ("y_hi", "x", "core")
CHIPS = AXES["x"] * AXES["y_hi"]
STEPS = (2, 1, 3)


def send(value, axis, step):
    size = AXES[axis]
    return lax.ppermute(value, axis, [(i, (i + step) % size) for i in range(size)])


def tied(*values):
    return lax.optimization_barrier(values)


def arrange_kernel(order_ref, inputs_ref, theirs_ref, gain_ref, scaled_ref):
    for j in range(CHIPS):
        start = pl.multiple_of(order_ref[j] * LANES, LANES)
        columns = pl.ds(start, LANES)
        gain = gain_ref[:, columns]
        for half, ref in enumerate((inputs_ref, theirs_ref)):
            scaled_ref[half, :, j * LANES : (j + 1) * LANES] = (
                ref[:, columns].astype(jnp.float32) * gain
            ).astype(jnp.bfloat16)


def feature_order():
    x, core = lax.axis_index("x"), lax.axis_index("core")
    rx, y = jnp.arange(CHIPS) // AXES["y_hi"], jnp.arange(CHIPS) % AXES["y_hi"]
    chip = y * AXES["x"] + (x + rx) % AXES["x"]
    return (chip * 2 + core).astype(jnp.int32)


def arrange(order, inputs, theirs, feature_gain):
    tokens, features = inputs.shape
    step = 96
    block = pl.BlockSpec((step, features), lambda i: (i, 0))
    scaled = pl.pallas_call(
        arrange_kernel,
        grid=(tokens // step,),
        out_shape=jax.ShapeDtypeStruct((2, tokens, features // 2), jnp.bfloat16),
        in_specs=[
            pl.BlockSpec(memory_space=pltpu.SMEM),
            block,
            block,
            pl.BlockSpec((1, features), lambda i: (0, 0)),
        ],
        out_specs=pl.BlockSpec((2, step, features // 2), lambda i: (0, i, 0)),
        compiler_params=pltpu.CompilerParams(vmem_limit_bytes=6 * VMEM_LIMIT),
        name="arrange",
    )(order, inputs, theirs, feature_gain[None, :])
    return scaled.reshape(2 * tokens, features // 2)


def exchange(parts, axis):
    return lax.all_to_all(parts, axis, split_axis=0, concat_axis=0, tiled=True)


def copies_of(value, axis):
    return jnp.broadcast_to(value[None], (lax.axis_size(axis), *value.shape))


def total(values):
    return functools.reduce(jnp.add, [value.astype(jnp.float32) for value in values])


def codes_kernel(global_ref, local_ref, decoded_ref):
    difference = global_ref[...].astype(jnp.float32) - local_ref[...].astype(jnp.float32)
    mean = jnp.mean(difference * difference, axis=-1, keepdims=True)
    scales = (clip_ratio * jnp.sqrt(mean + epsilon)).astype(jnp.bfloat16).astype(jnp.float32)
    codes = jnp.clip(difference / scales, -1.0, 1.0).astype(jnp.bfloat16)
    decoded_ref[...] = (codes.astype(jnp.float32) * scales).astype(jnp.bfloat16)


def fragment_codes(global_frag, local_frag):
    step = min(256, global_frag.shape[0])
    block = pl.BlockSpec((step, QBLOCK), lambda i: (i, 0))
    return pl.pallas_call(
        codes_kernel,
        grid=(global_frag.shape[0] // step,),
        out_shape=jax.ShapeDtypeStruct(global_frag.shape, jnp.bfloat16),
        in_specs=[block, block],
        out_specs=block,
        compiler_params=pltpu.CompilerParams(vmem_limit_bytes=VMEM_LIMIT),
        name="codes",
    )(global_frag, local_frag)


def update_kernel(replica_ref, arrived_ref, momentum_ref, global_ref, momentum_out, copies_ref):
    replicas = arrived_ref.shape[0]
    pseudo = total([arrived_ref[i] for i in range(replicas)]) / replicas
    new_momentum = outer_decay * momentum_ref[...] + pseudo
    momentum_out[...] = new_momentum
    own_next = (
        global_ref[...].astype(jnp.float32)
        - outer_rate * (pseudo + outer_decay * new_momentum)
    ).astype(jnp.bfloat16)
    for i in range(replicas):
        copies_ref[i] = own_next


def fragment_update(replica, arrived, global_frag, momentum):
    replicas, rows = arrived.shape[:2]
    shares = pl.BlockSpec((replicas, rows, QBLOCK), lambda i, replica: (0, 0, 0))
    share = pl.BlockSpec((rows, QBLOCK), lambda i, replica: (0, 0))
    return pl.pallas_call(
        update_kernel,
        grid_spec=pltpu.PrefetchScalarGridSpec(
            num_scalar_prefetch=1,
            grid=(1,),
            in_specs=[
                shares,
                share,
                pl.BlockSpec((rows, QBLOCK), lambda i, replica: (replica[0], 0)),
            ],
            out_specs=(share, shares),
        ),
        out_shape=(
            jax.ShapeDtypeStruct((rows, QBLOCK), jnp.float32),
            jax.ShapeDtypeStruct(arrived.shape, jnp.bfloat16),
        ),
        compiler_params=pltpu.CompilerParams(vmem_limit_bytes=VMEM_LIMIT),
        name="update",
    )(replica, arrived, momentum, global_frag)


def in_vmem(shape, dtype):
    return pltpu.VMEM(shape, dtype)


def product_kernel(scaled_ref, *refs):
    *weight_refs, partial_ref = refs
    group = weight_refs[0].shape[0]
    partial_ref[...] = total(
        [
            jnp.dot(
                scaled_ref[:, k * group : (k + 1) * group],
                ref[...],
                preferred_element_type=jnp.float32,
            )
            for k, ref in enumerate(weight_refs)
        ]
    )


def product(scaled, weights):
    return pl.pallas_call(
        product_kernel,
        out_shape=in_vmem((scaled.shape[0], weights[0].shape[1]), jnp.float32),
        in_specs=[WHOLE] * (1 + len(weights)),
        out_specs=WHOLE,
        compiler_params=pltpu.CompilerParams(vmem_limit_bytes=2 * VMEM_LIMIT),
        name="product",
    )(scaled, *weights)


def gradient_kernel(scaled_ref, mine_ref, theirs_ref, *refs):
    *target_refs, first, second, third, fourth, residual_ref = refs
    tokens = target_refs[0].shape[0]
    for half, target_ref in enumerate(target_refs):
        here = slice(half * tokens, (half + 1) * tokens)
        there = slice((1 - half) * tokens, (2 - half) * tokens)
        residual_ref[here, :] = (
            mine_ref[here, :] + theirs_ref[there, :] - target_ref[...].astype(jnp.float32)
        ).astype(jnp.bfloat16)
    group = first.shape[0]
    for k, ref in enumerate((first, second, third, fourth)):
        ref[...] = lax.dot_general(
            scaled_ref[:, k * group : (k + 1) * group],
            residual_ref[...],
            (((0,), (0,)), ((), ())),
            preferred_element_type=jnp.float32,
        ).astype(jnp.bfloat16)


def gradient_blocks(scaled, mine, theirs, targets):
    block = (scaled.shape[1] // AXES["x"], mine.shape[1])
    return pl.pallas_call(
        gradient_kernel,
        out_shape=(jax.ShapeDtypeStruct(block, jnp.bfloat16),) * AXES["x"],
        in_specs=[WHOLE] * 5,
        out_specs=(WHOLE,) * AXES["x"],
        scratch_shapes=[pltpu.VMEM(mine.shape, jnp.bfloat16)],
        compiler_params=pltpu.CompilerParams(vmem_limit_bytes=3 * VMEM_LIMIT),
        name="gradient",
    )(scaled, mine, theirs, *targets)


def add_kernel(first, second, third, fourth, sum_ref):
    sum_ref[...] = total([ref[...] for ref in (first, second, third, fourth)]).astype(
        jnp.bfloat16
    )


def add(blocks):
    return pl.pallas_call(
        add_kernel,
        out_shape=jax.ShapeDtypeStruct(blocks[0].shape, jnp.bfloat16),
        in_specs=[WHOLE] * 4,
        out_specs=WHOLE,
        compiler_params=pltpu.CompilerParams(vmem_limit_bytes=VMEM_LIMIT),
        name="add",
    )(*blocks)


def place_kernel(value_ref, placed_ref):
    placed_ref[...] = value_ref[...]


def place(value):
    step = value.shape[0] // 4
    block = pl.BlockSpec((step, value.shape[1]), lambda i: (i, 0))
    return pl.pallas_call(
        place_kernel,
        grid=(4,),
        out_shape=jax.ShapeDtypeStruct(value.shape, value.dtype),
        in_specs=[block],
        out_specs=block,
        compiler_params=pltpu.CompilerParams(vmem_limit_bytes=VMEM_LIMIT),
        name="place",
    )(value)


def collect_kernel(arrived_ref, gradient_ref, squares_ref):
    gradient = total([arrived_ref[k] for k in range(arrived_ref.shape[0])])
    gradient_ref[...] = gradient
    squares = jnp.sum(gradient * gradient, axis=0, keepdims=True)
    squares_ref[...] = jnp.broadcast_to(
        jnp.sum(squares, axis=1, keepdims=True), squares_ref.shape
    )


def collect(arrived):
    return pl.pallas_call(
        collect_kernel,
        out_shape=(
            jax.ShapeDtypeStruct(arrived.shape[1:], jnp.float32),
            jax.ShapeDtypeStruct((CHIPS * AXES["core"], LANES), jnp.float32),
        ),
        in_specs=[WHOLE],
        out_specs=(WHOLE, WHOLE),
        compiler_params=pltpu.CompilerParams(vmem_limit_bytes=VMEM_LIMIT),
        name="collect",
    )(arrived)


def clip_kernel(entries, squares_ref, gradient_ref, clipped_ref):
    mean_square = jnp.sum(squares_ref[...], axis=0, keepdims=True) / entries
    factor = jnp.minimum(1.0, lax.rsqrt(mean_square + epsilon))
    for j in range(gradient_ref.shape[1] // LANES):
        columns = slice(j * LANES, (j + 1) * LANES)
        clipped_ref[:, columns] = (gradient_ref[:, columns] * factor).astype(jnp.bfloat16)


def clip(squares, gradient, entries):
    return pl.pallas_call(
        functools.partial(clip_kernel, entries),
        out_shape=jax.ShapeDtypeStruct(gradient.shape, jnp.bfloat16),
        in_specs=[WHOLE, WHOLE],
        out_specs=WHOLE,
        compiler_params=pltpu.CompilerParams(vmem_limit_bytes=VMEM_LIMIT),
        name="clip",
    )(squares, gradient)


def shards(inputs, feature_gain, key_weight, teacher_keys, global_frag, local_frag, momentum):
    features = inputs.shape[2]
    rows, width = key_weight.shape[1:]
    replicas = lax.axis_size(REPLICA)
    replica = lax.axis_index(REPLICA).astype(jnp.int32)[None]
    global_frag = global_frag.reshape(-1, QBLOCK)
    local_frag = local_frag[0].reshape(-1, QBLOCK)
    momentum = momentum.reshape(-1, QBLOCK)
    key_weight, order, replica = tied(key_weight, feature_order(), replica)

    own, inputs, teacher_keys = tied(copies_of(key_weight[0], "y_hi"), inputs, teacher_keys)
    column = exchange(own, "y_hi").reshape(AXES["y_hi"] * rows, width)
    raw = send(inputs[0], "core", 1)
    targets = (teacher_keys[0], send(teacher_keys[0], "core", 1))
    scaled = arrange(order, inputs[0], raw, feature_gain)
    decoded = fragment_codes(global_frag, local_frag)
    column, scaled, targets, decoded, replica = tied(column, scaled, targets, decoded, replica)
    far = [column] + [send(column, "x", -k) for k in (1, 2, 3)]
    arrived = exchange(decoded.reshape(replicas, -1, QBLOCK), REPLICA)
    far, arrived = tied(far, arrived)
    partial = product(scaled, far)
    gradient = list(gradient_blocks(scaled, partial, send(partial, "core", 1), targets))
    gradient[0], arrived = tied(gradient[0], arrived)
    new_momentum, copies = fragment_update(replica, arrived, global_frag, momentum)
    new_global = exchange(copies, REPLICA)
    mine = add([gradient[0]] + [send(gradient[k], "x", k) for k in STEPS])
    mine, new_global = tied(mine, new_global)
    gradient, squares = collect(exchange(mine.reshape(AXES["y_hi"], rows, width), "y_hi"))

    squares, new_global = tied(squares, new_global)
    new_global = place(new_global.reshape(-1, QBLOCK))
    clipped_grad = clip(exchange(squares, FSDP), gradient, features * width)[None]
    return (clipped_grad, new_global.reshape(-1), new_momentum.reshape(-1))


def solution(mesh):
    parted = Mesh(mesh.devices.reshape(tuple(AXES.values())), tuple(AXES))
    return jax.shard_map(
        shards,
        mesh=parted,
        in_specs=(
            P(REPLICA, FSDP, None),
            P(),
            P(REPLICA, FSDP, None),
            P(REPLICA, FSDP, None),
            P(FSDP),
            P(REPLICA, FSDP),
            P(FSDP + REPLICA),
        ),
        out_specs=(P(REPLICA, FSDP, None), P(FSDP), P(FSDP + REPLICA)),
        check_vma=False,
    )
```
